128 devices in a mesh: lists: 32 (over x, z, core), sub: 4 (over y).
Axes of the slice: x: 4, y: 4, z: 4, core: 2. Of those that a mesh axis runs over, the one named last changes fastest.
Arguments:
- embeddings: bfloat16 [262144, 1024], P(('lists', 'sub')), may hold values from -6 to 6
- owner_of_row: int32 [262144, 1], P(('lists', 'sub')), may hold values from 0 to 31; in each aligned block of 2048 rows (0 to 2047, 2048 to 4095, ...) at most 128 rows name the same one
- list_in_owner: int32 [262144], P(('lists', 'sub')), may hold values from 0 to 2047
- opq_matrix: bfloat16 [1024, 1024], replicated, may hold values from -0.1875 to 0.1875
- centroids: bfloat16 [65536, 1024], P('lists', 'sub'), may hold values from -5 to 5
- codebook: bfloat16 [64, 16, 256], P('sub'), may hold values from -5 to 5
- code_targets: int32 [64, 524288], P('sub', 'lists'), may hold values from 0 to 255
Outputs:
- quant_error: float32 [64, 524288], P('sub', 'lists')
- new_codebook: float32 [64, 16, 256], P('sub')
The draws below stay inside these ranges and needn't reach their ends.
Inputs may be any that keep to these rules, and one draw needn't show every extreme that they name: `owner_of_row`: no more than 128 of the 2048 rows of one device name the same owner; some device sends exactly 128 rows to one owner.
All inputs are finite; a program needn't handle non-finite values.
Results may differ from the reference program's by a relative error of at most 0.0039.
Values may be sent and summed in bfloat16 or wider, within the bound.
No kernel may reach another device: no remote copies, remote signals or barrier semaphores. Data moves between devices by JAX's collectives and lax.ppermute only.
A program may use at most 128 MiB of HBM per device.

```python
import math
import jax
import jax.numpy as jnp
import numpy as np
from jax import lax

D = 1024
SUBDIM = 16
NSUBSP = 64
NCODE = 256
LIST_DEV = 2048
ROW_DEV = 2048
CAP = 128
TOKENS = 262144
NLIST = 65536
SLOTS = 524288
N_LISTS = 32
N_SUB = 4


def touch_ends(array, key, smallest, high):
    place = [jax.random.randint(jax.random.fold_in(key, axis), (), 0, length) for axis, length in enumerate(array.shape)]
    longest = array.shape.index(max(array.shape))
    next_to = place[:longest] + [(place[longest] + 1) % array.shape[longest]] + place[longest + 1:]
    return array.at[tuple(place)].set(smallest).at[tuple(next_to)].set(high)


def level_of(own_key, shape, pieces, least, high):
    level, own = 1.0, jax.random.fold_in(own_key, 6)
    for position, blocks in pieces:
        draws = jnp.exp(jax.random.uniform(jax.random.fold_in(own, position), (blocks,), jnp.float32, least / len(pieces), high / len(pieces)))
        level = level * jnp.repeat(draws, shape[position] // blocks).reshape([-1 if axis == position else 1 for axis in range(len(shape))])
    return level


def rank_table(count, skew):
    weights = [(1 << 20) // math.isqrt(standing ** skew) + 1 for standing in range(1, count + 1)]
    deviation = 1 + sum(weights) // (1 << 30)
    return np.cumsum(np.array([max(1, weight // deviation) for weight in weights]))


def skewed_ids(own_key, dims, amount, lean):
    listing = rank_table(amount, lean)
    lot = jax.random.randint(jax.random.fold_in(own_key, 1), dims, 0, int(listing[amount - 1]))
    rank = jnp.searchsorted(jnp.asarray(listing, jnp.int32), lot, side="right")
    return jax.random.permutation(jax.random.fold_in(own_key, 2), amount)[rank].astype(jnp.int32)


def shared_out(stream_key, own, number, rows, count, top, limit, lean):
    sequence = jax.random.permutation(stream_key, count)
    heavy_load, usual = portions_of(count, rows * top, limit, lean, True), portions_of(count, rows * top, limit, lean, False)
    places = jnp.arange(count)

    def named(lengths, offset_by):
        used = int((lengths > 0).sum())
        fixed = max(1, used // 4)
        moved = fixed + (places - fixed + offset_by * (used - fixed)) % max(1, count - fixed)
        return jnp.zeros((count,), jnp.int32).at[sequence[jnp.where(places < fixed, places, moved)]].set(jnp.asarray(lengths, jnp.int32))

    lengths = jnp.where(number % 4 == 0, named(heavy_load, number // 4), named(usual, number - number // 4 - 1))
    mixed = jax.random.permutation(jax.random.fold_in(own, 3), count)
    source_of, receiver = mixed[0:count // 2 * 2:2], mixed[1:count // 2 * 2:2]
    margin = jnp.minimum(lengths[source_of] - 1, limit - lengths[receiver]) // 2
    margin = jnp.where((source_of == sequence[0]) | (receiver == sequence[0]) | (lengths[receiver] == 0), 0, jnp.maximum(margin, 0))
    moved = jax.random.randint(jax.random.fold_in(own, 4), (count // 2,), 0, 1 << 20) % (margin + 1)
    lengths = lengths.at[source_of].add(-moved).at[receiver].add(moved)
    labels = jnp.searchsorted(jnp.cumsum(lengths), jnp.arange(rows * top), side="right").astype(jnp.int32)
    listing = labels.reshape(top, rows).T
    listing = listing[jax.random.permutation(jax.random.fold_in(own, 1), rows)]
    offset_by = jax.random.randint(jax.random.fold_in(own, 2), (rows, 1), 0, top)
    return jnp.take_along_axis(listing, (jnp.arange(top)[None, :] + offset_by) % top, axis=1)


def portions_of(amount, total, reach, lean, full):
    portions = [(1 << 20) // math.isqrt(grade ** lean) + 1 for grade in range(1, amount + 1)]
    largest = reach if full else min(reach, max(-(-total // amount), total * portions[0] // sum(portions)))
    least = 1 if total - largest >= amount - 1 else 0
    given, rest = [largest] + [least] * (amount - 1), total - largest - least * (amount - 1)
    while rest > 0:
        candidates = [i for i in range(1, amount) if given[i] < largest] or [i for i in range(1, amount) if given[i] < reach]
        pool, left = sum([portions[i] for i in candidates]), rest
        for i in candidates:
            more = min(reach - given[i], max(1, left * portions[i] // pool), rest)
            given[i] = given[i] + more
            rest = rest - more
    return np.array(given)


def scatter_about(stream_key, extent, spread, bound, split=(), held_as=jnp.bfloat16):
    values = jax.random.normal(stream_key, extent, jnp.float32) * spread
    if len(split) > 0:
        values = level_of(stream_key, extent, split, -0.22, 0.18) * values
    return jnp.clip(values, min=-bound, max=bound).astype(held_as)


def setup_inputs(seed: int = 0) -> dict:
    key_of = jax.random.split(jax.random.key(seed), 8)
    embeddings = scatter_about(key_of[0], (TOKENS, D), 1.0, 6.0, ((0, 128),))
    owner_of_row_keys = jax.random.split(jax.random.fold_in(key_of[1], 1), TOKENS // ROW_DEV)
    owner_of_row_turns = jax.random.permutation(jax.random.fold_in(key_of[1], 3), TOKENS // ROW_DEV)
    owner_of_row = jax.vmap(lambda own, number: shared_out(jax.random.fold_in(key_of[1], 2), own, number, ROW_DEV, N_LISTS, 1, CAP, 2))(owner_of_row_keys, owner_of_row_turns).reshape((TOKENS, 1))
    list_in_owner = touch_ends(jax.random.randint(key_of[2], (TOKENS,), 0, LIST_DEV), jax.random.fold_in(key_of[2], 1), 0, LIST_DEV - 1).astype(jnp.int32)
    opq_matrix = scatter_about(key_of[3], (D, D), D ** -0.5, 0.1875)
    centroids = scatter_about(key_of[4], (NLIST, D), 0.7, 5.0, ((0, 32), (1, 4)))
    codebook = scatter_about(key_of[5], (NSUBSP, SUBDIM, NCODE), 1.0, 5.0, ((0, 4),))
    code_targets = touch_ends(skewed_ids(key_of[6], (NSUBSP, SLOTS), NCODE, 2), jax.random.fold_in(key_of[6], 3), 0, NCODE - 1).astype(jnp.int32)
    return {"embeddings": embeddings, "owner_of_row": owner_of_row, "list_in_owner": list_in_owner, "opq_matrix": opq_matrix, "centroids": centroids, "codebook": codebook, "code_targets": code_targets}


def reference(embeddings, owner_of_row, list_in_owner, opq_matrix, centroids, codebook, code_targets):
    devices = N_LISTS * N_SUB
    per_owner = N_SUB * N_LISTS * CAP
    rotated = jnp.dot(embeddings, opq_matrix, preferred_element_type=jnp.float32).astype(jnp.bfloat16)
    owner = owner_of_row[:, 0].reshape(devices, ROW_DEV)
    onehot = (owner[:, :, None] == jnp.arange(N_LISTS, dtype=jnp.int32)[None, None, :]).astype(jnp.int32)
    rank = jnp.sum((jnp.cumsum(onehot, axis=1) - onehot) * onehot, axis=2)
    source = jnp.arange(devices, dtype=jnp.int32)[:, None]
    slot = owner * per_owner + (source % N_SUB) * (N_LISTS * CAP) + (source // N_SUB) * CAP + rank
    slot = slot.reshape(-1).astype(jnp.int32)
    row_of_slot = jnp.full((SLOTS,), -1, jnp.int32).at[slot].set(jnp.arange(TOKENS, dtype=jnp.int32))
    list_global = (owner_of_row[:, 0] * LIST_DEV + list_in_owner).astype(jnp.int32)
    code_f = codebook.astype(jnp.float32)
    code_sq = jnp.sum(code_f * code_f, axis=1)
    code_iota = jnp.arange(NCODE, dtype=jnp.int32)

    def one_owner(owner_index):
        start = (owner_index * per_owner).astype(jnp.int32)
        index = lax.dynamic_slice_in_dim(row_of_slot, start, per_owner)
        live = index >= 0
        safe = jnp.maximum(index, 0)
        rows = rotated[safe].astype(jnp.float32)
        centre = centroids[list_global[safe]].astype(jnp.float32)
        resid = jnp.where(live[:, None], rows - centre, 0.0).astype(jnp.bfloat16)
        resid = resid.reshape(per_owner, NSUBSP, SUBDIM).transpose(1, 0, 2)
        codes = lax.dynamic_slice_in_dim(code_targets, start, per_owner, 1)

        def one_sub(items):
            part, book, book_sq, targets = items
            part_f = part.astype(jnp.float32)
            row_sq = jnp.sum(part_f * part_f, axis=1)
            dots = jnp.dot(part, book, preferred_element_type=jnp.float32)
            dist = row_sq[:, None] - 2.0 * dots + book_sq[None, :]
            error = jnp.where(live, jnp.min(dist, axis=1), 0.0)
            hot = ((targets[:, None] == code_iota[None, :]) & live[:, None]).astype(jnp.bfloat16)
            sums = jnp.dot(part.T, hot, preferred_element_type=jnp.float32)
            counts = jnp.sum(hot.astype(jnp.float32), axis=0)
            return error, sums, counts

        return lax.map(one_sub, (resid, codebook, code_sq, codes))

    errors, sums, counts = lax.map(one_owner, jnp.arange(N_LISTS, dtype=jnp.int32))
    quant_error = errors.transpose(1, 0, 2).reshape(NSUBSP, SLOTS)
    totals = jnp.sum(sums, axis=0)
    tallies = jnp.sum(counts, axis=0)
    new_codebook = (code_f + totals) / (1.0 + tallies[:, None, :])
    return quant_error, new_codebook
```

```python
import functools

import jax
import jax.numpy as jnp
from jax import lax
from jax.experimental import pallas as pl
from jax.experimental.pallas import tpu as pltpu
from jax.sharding import PartitionSpec as P

BF = jnp.bfloat16
F32 = jnp.float32
I32 = jnp.int32
I16 = jnp.int16
OWNERS = 32
GROUPS = 4
CAP = 128
ROWS = 2048
WIDTH = 1024
SOURCES = OWNERS * GROUPS
SLOTS = SOURCES * CAP
LISTS = 2048
CODES = 256
MIB = 2**20


def nn(a, b):
    return jnp.dot(a, b, preferred_element_type=F32)


def nt(a, b):
    return lax.dot_general(a, b, (((1,), (1,)), ((), ())), preferred_element_type=F32)


def params(mib=48):
    return pltpu.CompilerParams(
        vmem_limit_bytes=mib * MIB, dimension_semantics=("arbitrary",)
    )


def cost(flops, bytes_accessed):
    return pl.CostEstimate(
        flops=int(flops), bytes_accessed=int(bytes_accessed), transcendentals=0
    )


def rank_kernel(owner_ref, list_ref, slot_ref, ids_ref):
    owner = owner_ref[...]
    lists = list_ref[...]
    owner_hot = (owner == lax.broadcasted_iota(I32, (OWNERS, ROWS), 0)).astype(F32)
    before = (
        lax.broadcasted_iota(I32, (128, 128), 0) < lax.broadcasted_iota(I32, (128, 128), 1)
    ).astype(F32).astype(BF)
    blocks = ROWS // 128
    stacked = jnp.concatenate(
        [owner_hot[:, b * 128 : (b + 1) * 128] for b in range(blocks)], axis=0
    ).astype(BF)
    inside = nn(stacked, before)
    ranks = []
    carry = jnp.zeros((OWNERS, 1), F32)
    for b in range(blocks):
        hot = owner_hot[:, b * 128 : (b + 1) * 128]
        earlier = inside[b * OWNERS : (b + 1) * OWNERS] + carry
        ranks.append(jnp.sum(hot * earlier, axis=0, keepdims=True))
        carry = carry + jnp.sum(hot, axis=1, keepdims=True)
    rank = jnp.concatenate(ranks, axis=1).astype(I32)
    slot_ref[...] = owner * CAP + rank
    rank_hot = (rank == lax.broadcasted_iota(I32, (CAP, ROWS), 0)).astype(F32).astype(BF)
    high = (lists // 128).astype(F32)
    low = (lists % 128).astype(F32)
    left = jnp.concatenate([owner_hot * high, owner_hot * low, owner_hot], axis=0).astype(BF)
    found = nt(left, rank_hot)
    number = found[:OWNERS] * 128.0 + found[OWNERS : 2 * OWNERS]
    live = found[2 * OWNERS :]
    ids_ref[...] = (number + live - 1.0).astype(I32)


def rank_rows(owner, lists):
    return pl.pallas_call(
        rank_kernel,
        out_shape=[
            jax.ShapeDtypeStruct((1, ROWS), I32),
            jax.ShapeDtypeStruct((OWNERS, CAP), I32),
        ],
        compiler_params=pltpu.CompilerParams(vmem_limit_bytes=32 * MIB),
        cost_estimate=cost(1e9, 100000),
    )(owner, lists)


def route_kernel(step_owners, slot_ref, rows_ref, r0, r1, r2, r3, out_ref, rot_ref):
    step = pl.program_id(0)

    @pl.when(step == 0)
    def _():
        for g, r in enumerate((r0, r1, r2, r3)):
            rot_ref[:, g * 128 : (g + 1) * 128] = nn(rows_ref[...], r[...]).astype(BF)

    count = step_owners * CAP
    place = slot_ref[...] - step * count
    hot = (place == lax.broadcasted_iota(I32, (count, ROWS), 0)).astype(F32).astype(BF)
    sent = nn(hot, rot_ref[...]).astype(BF)
    for g in range(GROUPS):
        part = sent[:, g * 128 : (g + 1) * 128]
        out_ref[g] = part.reshape(step_owners, CAP, 128)


def route(half, slot, embeddings, matrix):
    step_owners = 4
    columns = [
        pl.BlockSpec((WIDTH, 128), functools.partial(lambda col, i: (0, col), 2 * g + half))
        for g in range(GROUPS)
    ]
    return pl.pallas_call(
        functools.partial(route_kernel, step_owners),
        grid=(OWNERS // step_owners,),
        in_specs=[
            pl.BlockSpec((1, ROWS), lambda i: (0, 0)),
            pl.BlockSpec((ROWS, WIDTH), lambda i: (0, 0)),
            *columns,
        ],
        out_specs=pl.BlockSpec((GROUPS, step_owners, CAP, 128), lambda i: (0, i, 0, 0)),
        out_shape=jax.ShapeDtypeStruct((GROUPS, OWNERS, CAP, 128), BF),
        scratch_shapes=[pltpu.VMEM((ROWS, GROUPS * 128), BF)],
        compiler_params=params(),
        cost_estimate=cost(11e9, 10 * MIB),
    )(slot, embeddings, matrix, matrix, matrix, matrix)


def pick_kernel(step_sources, ids_ref, centroid_ref, target_ref, out_ref, count_ref, acc_ref):
    step = pl.program_id(0)

    @pl.when(step == 0)
    def _():
        acc_ref[...] = jnp.zeros_like(acc_ref)

    slots = step_sources * CAP
    one = jnp.ones((), BF)
    zero = jnp.zeros((), BF)
    lane = lax.broadcasted_iota(I32, (CAP, 128), 1).astype(I16)
    for j in range(step_sources):
        ids = ids_ref[j : j + 1, :].astype(F32)
        column = jnp.broadcast_to(ids, (128, CAP)).T.astype(I32).astype(I16)
        hot = jnp.concatenate(
            [
                jnp.where(column == lane + jnp.int16(128 * b), one, zero)
                for b in range(LISTS // 128)
            ],
            axis=1,
        )
        out_ref[j] = nn(hot, centroid_ref[...]).astype(BF)

    live = jnp.concatenate([ids_ref[j : j + 1, :] for j in range(step_sources)], axis=1) >= 0
    target = jnp.where(live, target_ref[...], -1)
    high = jnp.where(live, target // 16, -1).astype(I16)
    low = (target % 16).astype(I16)
    digit = lax.broadcasted_iota(I32, (16, slots), 0).astype(I16)
    left = []
    right = []
    for m in range(16):
        left.append(jnp.where(high[m : m + 1] == digit, one, zero))
        right.append(jnp.where(low[m : m + 1] == digit, one, zero))
    acc_ref[...] += nt(jnp.concatenate(left, axis=0), jnp.concatenate(right, axis=0))

    @pl.when(step == pl.num_programs(0) - 1)
    def _():
        for m in range(16):
            block = acc_ref[m * 16 : (m + 1) * 16, m * 16 : (m + 1) * 16]
            count_ref[m] = block


def pick(ids, centroids, targets):
    step_sources = 8
    slots = step_sources * CAP
    return pl.pallas_call(
        functools.partial(pick_kernel, step_sources),
        grid=(SOURCES // step_sources,),
        in_specs=[
            pl.BlockSpec((step_sources, CAP), lambda i: (i, 0)),
            pl.BlockSpec((LISTS, 256), lambda i: (0, 0)),
            pl.BlockSpec((16, slots), lambda i: (0, i)),
        ],
        out_specs=[
            pl.BlockSpec((step_sources, CAP, 256), lambda i: (i, 0, 0)),
            pl.BlockSpec((16, 16, 16), lambda i: (0, 0, 0)),
        ],
        out_shape=[
            jax.ShapeDtypeStruct((SOURCES, CAP, 256), BF),
            jax.ShapeDtypeStruct((16, 16, 16), F32),
        ],
        scratch_shapes=[pltpu.VMEM((256, 256), F32)],
        compiler_params=params(),
        cost_estimate=cost(20e9, 12 * MIB),
    )(ids, centroids, targets)


def book_kernel(code_ref, out_ref):
    codes = code_ref[...].astype(F32).T
    lane = lax.broadcasted_iota(I32, (CODES, 128), 1)
    for m in range(8):
        mine = jnp.where(lane // 16 == m, codes, 0.0)
        square = jnp.sum(mine * mine, axis=1, keepdims=True)
        high = square.astype(BF).astype(F32)
        middle = (square - high).astype(BF).astype(F32)
        low = square - high - middle
        tail = jnp.where(
            lane == 0, high, jnp.where(lane == 1, middle, jnp.where(lane == 2, low, 0.0))
        )
        out_ref[m * CODES : (m + 1) * CODES, :128] = (-2.0 * mine).astype(BF)
        out_ref[m * CODES : (m + 1) * CODES, 128:] = tail.astype(BF)


def make_book(codebook):
    return pl.pallas_call(
        book_kernel,
        grid=(2,),
        in_specs=[pl.BlockSpec((128, CODES), lambda i: (i, 0))],
        out_specs=pl.BlockSpec((8 * CODES, 256), lambda i: (i, 0)),
        out_shape=jax.ShapeDtypeStruct((16 * CODES, 256), BF),
        compiler_params=params(),
        cost_estimate=cost(1e9, 3 * MIB),
    )(codebook.reshape(256, CODES))


def residual(rows_ref, pick_ref, slots):
    rows = rows_ref[...].reshape(slots, 128).astype(F32)
    centre = pick_ref[...].reshape(slots, 128).astype(F32)
    return (rows - centre).astype(BF)


def sums_kernel(slots, rows_ref, pick_ref, target_ref, out_ref, acc_ref):
    step = pl.program_id(0)

    @pl.when(step == 0)
    def _():
        acc_ref[...] = jnp.zeros_like(acc_ref)

    flipped = residual(rows_ref, pick_ref, slots).astype(F32).T.astype(BF)
    target = target_ref[...]
    high = (target // 64).astype(I16)
    low = (target % 64).astype(I16)
    digit = lax.broadcasted_iota(I32, (64, slots), 0).astype(I16)
    one = jnp.ones((), BF)
    zero = jnp.zeros((), BF)
    for t in range(2):
        left = []
        right = []
        for m in range(4 * t, 4 * t + 4):
            mine = flipped[m * 16 : (m + 1) * 16]
            row = jnp.broadcast_to(high[m : m + 1], (16, slots))
            for h in range(4):
                left.append(jnp.where(row == jnp.int16(h), mine, zero))
            right.append(jnp.where(low[m : m + 1] == digit, one, zero))
        acc_ref[t] += nt(jnp.concatenate(left, axis=0), jnp.concatenate(right, axis=0))

    @pl.when(step == pl.num_programs(0) - 1)
    def _():
        for m in range(8):
            part = acc_ref[m // 4][:, (m % 4) * 64 : (m % 4 + 1) * 64]
            base = (m % 4) * 64
            out_ref[m] = jnp.concatenate(
                [part[base + h * 16 : base + (h + 1) * 16] for h in range(4)], axis=1
            )


def code_sums(half, rows, picked, targets):
    step_sources = 16
    slots = step_sources * CAP
    return pl.pallas_call(
        functools.partial(sums_kernel, slots),
        grid=(SOURCES // step_sources,),
        in_specs=[
            pl.BlockSpec((step_sources, CAP, 128), lambda i: (i, 0, 0)),
            pl.BlockSpec((step_sources, CAP, 128), lambda i: (i, 0, half)),
            pl.BlockSpec((8, slots), lambda i: (half, i)),
        ],
        out_specs=pl.BlockSpec((8, 16, CODES), lambda i: (0, 0, 0)),
        out_shape=jax.ShapeDtypeStruct((8, 16, CODES), F32),
        scratch_shapes=[pltpu.VMEM((2, 256, 256), F32)],
        compiler_params=params(),
        cost_estimate=cost(4e9, 9 * MIB),
    )(rows, picked, targets)


def errors_kernel(slots, rows_ref, pick_ref, ids_ref, book_ref, out_ref):
    resid = residual(rows_ref, pick_ref, slots)
    wide = jnp.concatenate([resid, jnp.ones((slots, 128), BF)], axis=1)
    square = resid.astype(F32) * resid.astype(F32)
    high = square.astype(BF)
    low = (square - high.astype(F32)).astype(BF)
    member = (
        (lax.broadcasted_iota(I32, (16, 256), 1) % 128) // 16
        == lax.broadcasted_iota(I32, (16, 256), 0)
    ).astype(F32).astype(BF)
    row_sq = nt(member, jnp.concatenate([high, low], axis=1))
    sources = slots // CAP
    live = jnp.concatenate([ids_ref[j : j + 1, :] for j in range(sources)], axis=1) >= 0
    for m in range(8):
        dist = nt(book_ref[m * CODES : (m + 1) * CODES], wide)
        least = jnp.min(dist, axis=0, keepdims=True)
        out_ref[m : m + 1, :] = jnp.where(live, row_sq[m : m + 1] + least, 0.0)


def errors(half, rows, picked, ids, book):
    step_sources = 16
    slots = step_sources * CAP
    return pl.pallas_call(
        functools.partial(errors_kernel, slots),
        grid=(SOURCES // step_sources,),
        in_specs=[
            pl.BlockSpec((step_sources, CAP, 128), lambda i: (i, 0, 0)),
            pl.BlockSpec((step_sources, CAP, 128), lambda i: (i, 0, half)),
            pl.BlockSpec((step_sources, CAP), lambda i: (i, 0)),
            pl.BlockSpec((8 * CODES, 256), lambda i: (half, 0)),
        ],
        out_specs=pl.BlockSpec((8, slots), lambda i: (0, i)),
        out_shape=jax.ShapeDtypeStruct((8, SLOTS), F32),
        compiler_params=params(),
        cost_estimate=cost(18e9, 9 * MIB),
    )(rows, picked, ids, book)


def exchange(x, axes):
    return lax.all_to_all(x, axes, split_axis=0, concat_axis=0, tiled=True)


def per_device(
    embeddings, owner_of_row, list_in_owner, opq_matrix, centroids, codebook, code_targets
):
    every = ("sub", "lists")
    slot, ids = rank_rows(owner_of_row.reshape(1, ROWS), list_in_owner.reshape(1, ROWS))
    send_ids = jnp.broadcast_to(ids[None, :, None, :], (GROUPS, OWNERS, 1, CAP))
    got_ids = exchange(send_ids.reshape(SOURCES, 1, CAP), every).reshape(SOURCES, CAP)
    first = route(0, slot, embeddings, opq_matrix).reshape(SOURCES, CAP, 128)
    rows0 = exchange(first, every)
    second = route(1, slot, embeddings, opq_matrix).reshape(SOURCES, CAP, 128)
    book = make_book(codebook)
    picked, counts = pick(got_ids, centroids, code_targets)
    rows1 = exchange(second, every)
    sums0 = code_sums(0, rows0, picked, code_targets)
    errors0 = errors(0, rows0, picked, got_ids, book)
    sums1 = code_sums(1, rows1, picked, code_targets)
    sums = jnp.concatenate([sums0, sums1], axis=0)
    pieces = jnp.concatenate(
        [
            sums.reshape(16, 16, 2, 128).transpose(0, 2, 1, 3).reshape(OWNERS, 16, 128),
            jnp.broadcast_to(counts.reshape(OWNERS, 1, 128), (OWNERS, 8, 128)),
        ],
        axis=1,
    )
    got = jnp.sum(exchange(pieces, "lists"), axis=0)
    errors1 = errors(1, rows1, picked, got_ids, book)
    me = lax.axis_index("lists")
    code_piece = lax.dynamic_slice(codebook, (me // 2, 0, (me % 2) * 128), (1, 16, 128))[0]
    new_piece = (code_piece.astype(F32) + got[:16]) / (1.0 + got[16:17])
    spread = exchange(jnp.broadcast_to(new_piece[None], (OWNERS, 16, 128)), "lists")
    new_codebook = (
        spread.reshape(16, 2, 16, 128).transpose(0, 2, 1, 3).reshape(16, 16, CODES)
    )
    quant_error = jnp.concatenate([errors0, errors1], axis=0)
    return quant_error, new_codebook


def solution(mesh):
    placed = (
        P(("lists", "sub"), None),
        P(("lists", "sub"), None),
        P(("lists", "sub")),
        P(),
        P("lists", "sub"),
        P("sub", None, None),
        P("sub", "lists"),
    )
    return jax.shard_map(
        per_device,
        mesh=mesh,
        in_specs=placed,
        out_specs=(P("sub", "lists"), P("sub", None, None)),
        check_vma=False,
    )
```

```python
import functools

import jax
import jax.numpy as jnp
from jax import lax
from jax.experimental import pallas as pl
from jax.experimental.pallas import tpu as pltpu
from jax.sharding import PartitionSpec as P

BF = jnp.bfloat16
F32 = jnp.float32
I32 = jnp.int32
I16 = jnp.int16
OWNERS = 32
GROUPS = 4
CAP = 128
ROWS = 2048
WIDTH = 1024
SOURCES = OWNERS * GROUPS
SLOTS = SOURCES * CAP
LISTS = 2048
CODES = 256
MIB = 2**20


def nn(a, b):
    return jnp.dot(a, b, preferred_element_type=F32)


def nt(a, b):
    return lax.dot_general(a, b, (((1,), (1,)), ((), ())), preferred_element_type=F32)


def params(mib):
    return pltpu.CompilerParams(
        vmem_limit_bytes=mib * MIB, dimension_semantics=("arbitrary",)
    )


def cost(flops, bytes_accessed):
    return pl.CostEstimate(
        flops=int(flops), bytes_accessed=int(bytes_accessed), transcendentals=0
    )


def rank_kernel(owner_ref, list_ref, place_ref, start_ref, ids_ref):
    owner = owner_ref[...]
    lists = list_ref[...]
    owner_hot = (owner == lax.broadcasted_iota(I32, (OWNERS, ROWS), 0)).astype(F32)
    before = (
        lax.broadcasted_iota(I32, (128, 128), 0) < lax.broadcasted_iota(I32, (128, 128), 1)
    ).astype(F32).astype(BF)
    blocks = ROWS // 128
    stacked = jnp.concatenate(
        [owner_hot[:, b * 128 : (b + 1) * 128] for b in range(blocks)], axis=0
    ).astype(BF)
    inside = nn(stacked, before)
    ranks = []
    carry = jnp.zeros((OWNERS, 1), F32)
    for b in range(blocks):
        hot = owner_hot[:, b * 128 : (b + 1) * 128]
        earlier = inside[b * OWNERS : (b + 1) * OWNERS] + carry
        ranks.append(jnp.sum(hot * earlier, axis=0, keepdims=True))
        carry = carry + jnp.sum(hot, axis=1, keepdims=True)
    rank = jnp.concatenate(ranks, axis=1)
    pages = ((carry.astype(I32) + 15) // 16).astype(F32).astype(BF)
    first = nn(before[:OWNERS, :OWNERS].astype(F32).T.astype(BF), jnp.broadcast_to(pages, (OWNERS, 128)))
    begin = jnp.sum(owner_hot * first[:, :1], axis=0, keepdims=True) * 16.0
    place_ref[...] = (begin + rank).astype(I32)
    start_ref[...] = first.astype(I32)
    rank_hot = (rank.astype(I32) == lax.broadcasted_iota(I32, (CAP, ROWS), 0)).astype(F32).astype(BF)
    high = (lists // 128).astype(F32)
    low = (lists % 128).astype(F32)
    left = jnp.concatenate([owner_hot * high, owner_hot * low, owner_hot], axis=0).astype(BF)
    found = nt(left, rank_hot)
    number = found[:OWNERS] * 128.0 + found[OWNERS : 2 * OWNERS]
    live = found[2 * OWNERS :]
    ids_ref[...] = (number + live - 1.0).astype(I32)


def rank_rows(owner, lists):
    return pl.pallas_call(
        rank_kernel,
        out_shape=[
            jax.ShapeDtypeStruct((1, ROWS), I32),
            jax.ShapeDtypeStruct((OWNERS, 128), I32),
            jax.ShapeDtypeStruct((OWNERS, CAP), I32),
        ],
        compiler_params=pltpu.CompilerParams(vmem_limit_bytes=56 * MIB),
        cost_estimate=cost(1e9, 100000),
    )(owner, lists)


ORDERED = ROWS + 16 * OWNERS
ID_ROWS = 16
HALF = CAP // 2
HALF_SLOTS = SOURCES * HALF


def order_rows(step, rot_steps, row_steps, place_ref, rows_ref, columns, rot_ref, run_ref):
    rot_rows = ROWS // rot_steps
    run_rows = ORDERED // row_steps

    @pl.when(step < rot_steps)
    def _():
        matrix = jnp.concatenate([r[...] for r in columns], axis=1)
        at = pl.multiple_of(step * rot_rows, rot_rows)
        rot_ref[pl.ds(at, rot_rows), :] = nn(rows_ref[...], matrix).astype(BF)

    @pl.when(step == 0)
    def _():
        run_ref[ORDERED:, :] = jnp.zeros((CAP, GROUPS * 128), BF)

    @pl.when(step == rot_steps)
    def _():
        one = jnp.ones((), BF)
        zero = jnp.zeros((), BF)
        digit = lax.broadcasted_iota(I32, (run_rows, ROWS), 0).astype(I16)
        for k in range(row_steps):
            place = (place_ref[...] - k * run_rows).astype(I16)
            hot = jnp.where(place == digit, one, zero)
            run_ref[k * run_rows : (k + 1) * run_rows, :] = nn(hot, rot_ref[...]).astype(BF)


def first_route_kernel(rot_steps, row_steps, step_owners, start_ref, place_ref, ids_ref, rows_ref,
                       r0, r1, r2, r3, low_ref, high_ref, rot_ref, run_ref):
    step = pl.program_id(0)
    order_rows(step, rot_steps, row_steps, place_ref, rows_ref, (r0, r1, r2, r3), rot_ref, run_ref)

    @pl.when(step >= rot_steps)
    def _():
        line = lax.broadcasted_iota(I32, (ID_ROWS, CAP), 0)
        for j in range(step_owners):
            owner = (step - rot_steps) * step_owners + j
            begin = pl.multiple_of(start_ref[owner, 0] * 16, 16)
            run = run_ref[pl.ds(begin, CAP), :]
            ids = ids_ref[pl.ds(owner, 1), :]
            high = jnp.where(ids < 0, -1, ids // 128)
            low = ids % 128
            tail = jnp.where(line == 0, high, jnp.where(line == 1, low, 0))
            tail = tail.astype(F32).astype(BF)
            for g in range(GROUPS):
                low_ref[g, j, :HALF, :] = run[:HALF, g * 128 : (g + 1) * 128]
                low_ref[g, j, HALF:, :] = tail
                high_ref[g, j] = run[HALF:, g * 128 : (g + 1) * 128]


def second_route_kernel(rot_steps, row_steps, step_owners, start_ref, place_ref, rest_ref, rows_ref,
                        r0, r1, r2, r3, both_ref, high_ref, rot_ref, run_ref):
    step = pl.program_id(0)
    order_rows(step, rot_steps, row_steps, place_ref, rows_ref, (r0, r1, r2, r3), rot_ref, run_ref)

    @pl.when(step >= rot_steps)
    def _():
        for j in range(step_owners):
            owner = (step - rot_steps) * step_owners + j
            begin = pl.multiple_of(start_ref[owner, 0] * 16, 16)
            run = run_ref[pl.ds(begin, CAP), :]
            for g in range(GROUPS):
                both_ref[g, j, :HALF, :] = rest_ref[g, j]
                both_ref[g, j, HALF:, :] = run[:HALF, g * 128 : (g + 1) * 128]
                high_ref[g, j] = run[HALF:, g * 128 : (g + 1) * 128]


def route(half, start, place, extra, embeddings, matrix):
    step_owners = 8
    rot_steps = 2
    row_steps = 5
    depths = (HALF + ID_ROWS, HALF) if half == 0 else (CAP, HALF)
    columns = [
        pl.BlockSpec((WIDTH, 128), functools.partial(lambda col, i: (0, col), 2 * g + half))
        for g in range(GROUPS)
    ]

    def by_owner(i):
        return (0, jnp.maximum(i - rot_steps, 0), 0, 0)

    if half == 0:
        extra_spec = pl.BlockSpec((OWNERS, CAP), lambda i: (0, 0))
    else:
        extra_spec = pl.BlockSpec((GROUPS, step_owners, HALF, 128), by_owner)
    kernel = first_route_kernel if half == 0 else second_route_kernel
    return pl.pallas_call(
        functools.partial(kernel, rot_steps, row_steps, step_owners),
        grid=(rot_steps + OWNERS // step_owners,),
        in_specs=[
            pl.BlockSpec(memory_space=pltpu.SMEM),
            pl.BlockSpec((1, ROWS), lambda i: (0, 0)),
            extra_spec,
            pl.BlockSpec((ROWS // rot_steps, WIDTH), lambda i: (jnp.minimum(i, rot_steps - 1), 0)),
            *columns,
        ],
        out_specs=[pl.BlockSpec((GROUPS, step_owners, d, 128), by_owner) for d in depths],
        out_shape=[jax.ShapeDtypeStruct((GROUPS, OWNERS, d, 128), BF) for d in depths],
        scratch_shapes=[
            pltpu.VMEM((ROWS, GROUPS * 128), BF),
            pltpu.VMEM((ORDERED + CAP, GROUPS * 128), BF),
        ],
        compiler_params=params(56),
        cost_estimate=cost(8e9, 10 * MIB),
    )(start, place, extra, embeddings, matrix, matrix, matrix, matrix)


def pick_kernel(step_sources, tail_ref, centroid_ref, target_ref, out_ref, lower_ref, upper_ref, count_ref, acc_ref):
    step = pl.program_id(0)

    @pl.when(step == 0)
    def _():
        acc_ref[...] = jnp.zeros_like(acc_ref)

    slots = step_sources * CAP
    one = jnp.ones((), BF)
    zero = jnp.zeros((), BF)
    lane = lax.broadcasted_iota(I32, (CAP, 128), 1).astype(I16)
    numbers = []
    hots = []
    for j in range(step_sources):
        tail = tail_ref[j].astype(F32)
        number = tail[0:1, :] * 128.0 + tail[1:2, :]
        numbers.append(number)
        column = jnp.broadcast_to(number, (128, CAP)).T.astype(I32).astype(I16)
        hots.append(
            jnp.concatenate(
                [
                    jnp.where(column == lane + jnp.int16(128 * b), one, zero)
                    for b in range(LISTS // 128)
                ],
                axis=1,
            )
        )
    found = nn(jnp.concatenate(hots, axis=0), centroid_ref[...]).astype(BF)
    out_ref[...] = found.reshape(step_sources, CAP, 256)
    side = lax.broadcasted_iota(I32, (1, CAP), 1) < HALF
    lower = []
    upper = []
    for j in range(0, step_sources, 2):
        even, odd = numbers[j], numbers[j + 1]
        lower.append(jnp.where(side, even, pltpu.roll(odd, HALF, 1)))
        upper.append(jnp.where(side, pltpu.roll(even, HALF, 1), odd))
    lower_ref[...] = jnp.concatenate(lower, axis=1)
    upper_ref[...] = jnp.concatenate(upper, axis=1)

    live = jnp.concatenate(numbers, axis=1) >= 0
    target = jnp.where(live, target_ref[...], -1)
    high = jnp.where(live, target // 16, -1).astype(I16)
    low = (target % 16).astype(I16)
    digit = lax.broadcasted_iota(I32, (16, slots), 0).astype(I16)
    left = []
    right = []
    for m in range(16):
        left.append(jnp.where(high[m : m + 1] == digit, one, zero))
        right.append(jnp.where(low[m : m + 1] == digit, one, zero))
    acc_ref[...] += nt(jnp.concatenate(left, axis=0), jnp.concatenate(right, axis=0))

    @pl.when(step == pl.num_programs(0) - 1)
    def _():
        for m in range(16):
            block = acc_ref[m * 16 : (m + 1) * 16, m * 16 : (m + 1) * 16]
            count_ref[m] = block


def pick(rows0, centroids, targets):
    step_sources = 16
    slots = step_sources * CAP
    return pl.pallas_call(
        functools.partial(pick_kernel, step_sources),
        grid=(SOURCES // step_sources,),
        in_specs=[
            pl.BlockSpec((step_sources, ID_ROWS, CAP), lambda i: (i, HALF // ID_ROWS, 0)),
            pl.BlockSpec((LISTS, 256), lambda i: (0, 0)),
            pl.BlockSpec((16, slots), lambda i: (0, i)),
        ],
        out_specs=[
            pl.BlockSpec((step_sources, CAP, 256), lambda i: (i, 0, 0)),
            pl.BlockSpec((1, slots // 2), lambda i: (0, i)),
            pl.BlockSpec((1, slots // 2), lambda i: (0, i)),
            pl.BlockSpec((16, 16, 16), lambda i: (0, 0, 0)),
        ],
        out_shape=[
            jax.ShapeDtypeStruct((SOURCES, CAP, 256), BF),
            jax.ShapeDtypeStruct((1, HALF_SLOTS), F32),
            jax.ShapeDtypeStruct((1, HALF_SLOTS), F32),
            jax.ShapeDtypeStruct((16, 16, 16), F32),
        ],
        scratch_shapes=[pltpu.VMEM((256, 256), F32)],
        compiler_params=params(56),
        cost_estimate=cost(20e9, 12 * MIB),
    )(rows0, centroids, targets)


def book_kernel(code_ref, out_ref):
    codes = code_ref[...].astype(F32).T
    lane = lax.broadcasted_iota(I32, (CODES, 128), 1)
    for m in range(8):
        mine = jnp.where(lane // 16 == m, codes, 0.0)
        square = jnp.sum(mine * mine, axis=1, keepdims=True)
        high = square.astype(BF).astype(F32)
        middle = (square - high).astype(BF).astype(F32)
        low = square - high - middle
        tail = jnp.where(
            lane == 0, high, jnp.where(lane == 1, middle, jnp.where(lane == 2, low, 0.0))
        )
        out_ref[m * CODES : (m + 1) * CODES, :128] = (-2.0 * mine).astype(BF)
        out_ref[m * CODES : (m + 1) * CODES, 128:] = tail.astype(BF)


def make_book(codebook):
    return pl.pallas_call(
        book_kernel,
        grid=(2,),
        in_specs=[pl.BlockSpec((128, CODES), lambda i: (i, 0))],
        out_specs=pl.BlockSpec((8 * CODES, 256), lambda i: (i, 0)),
        out_shape=jax.ShapeDtypeStruct((16 * CODES, 256), BF),
        compiler_params=params(56),
        cost_estimate=cost(1e9, 3 * MIB),
    )(codebook.reshape(256, CODES))


def residual(rows_ref, pick_ref, slots):
    rows = rows_ref[...].reshape(slots, 128).astype(F32)
    centre = pick_ref[...].reshape(slots, 128).astype(F32)
    return (rows - centre).astype(BF)


def add_sums(slots, flipped, live, target, acc_ref):
    high = jnp.where(live, target // 64, -1).astype(I16)
    low = (target % 64).astype(I16)
    digit = lax.broadcasted_iota(I32, (64, slots), 0).astype(I16)
    one = jnp.ones((), BF)
    zero = jnp.zeros((), BF)
    for t in range(2):
        left = []
        right = []
        for m in range(4 * t, 4 * t + 4):
            mine = flipped[m * 16 : (m + 1) * 16]
            row = jnp.broadcast_to(high[m : m + 1], (16, slots))
            for h in range(4):
                left.append(jnp.where(row == jnp.int16(h), mine, zero))
            right.append(jnp.where(low[m : m + 1] == digit, one, zero))
        acc_ref[t] += nt(jnp.concatenate(left, axis=0), jnp.concatenate(right, axis=0))


def sum_of(acc_ref, m):
    base = (m % 4) * 64
    part = acc_ref[m // 4][:, base : base + 64]
    return jnp.concatenate([part[base + h * 16 : base + (h + 1) * 16] for h in range(4)], axis=1)


def least_errors(slots, resid, flipped, live, book_ref):
    wide = jnp.concatenate([resid, jnp.ones((slots, 128), BF)], axis=1)
    lines = []
    for m in range(8):
        mine = flipped[m * 16 : (m + 1) * 16]
        row_sq = jnp.sum(mine * mine, axis=0, keepdims=True)
        dist = nt(book_ref[m * CODES : (m + 1) * CODES], wide)
        least = jnp.min(dist, axis=0, keepdims=True)
        lines.append(jnp.where(live, row_sq + least, 0.0))
    return lines


def quarter_kernel(slots, rows_ref, pick_ref, ids_ref, target_ref, book_ref, error_ref, sum_ref, acc_ref):
    step = pl.program_id(0)

    @pl.when(step == 0)
    def _():
        acc_ref[...] = jnp.zeros_like(acc_ref)

    resid = residual(rows_ref, pick_ref, slots)
    flipped = resid.astype(F32).T
    live = ids_ref[...] >= 0
    add_sums(slots, flipped.astype(BF), live, target_ref[0], acc_ref)
    for m, line in enumerate(least_errors(slots, resid, flipped, live, book_ref)):
        error_ref[m : m + 1, :] = line

    @pl.when(step == pl.num_programs(0) - 1)
    def _():
        for m in range(8):
            sum_ref[m] = sum_of(acc_ref, m)


def quarter_specs(step_sources, half, side, place, begin=0):
    slots = step_sources * HALF
    return [
        pl.BlockSpec((step_sources, HALF, 128), lambda i: (i + begin, place, 0)),
        pl.BlockSpec((step_sources, HALF, 128), lambda i: (i + begin, side, half)),
        pl.BlockSpec((1, slots), lambda i: (0, i + begin)),
        pl.BlockSpec((1, 8, slots), lambda i: (side, half, i + begin)),
        pl.BlockSpec((8 * CODES, 256), lambda i: (half, 0)),
    ]


def quarter(half, side, place, rows, picked, ids, targets, book):
    step_sources = 32
    slots = step_sources * HALF
    return pl.pallas_call(
        functools.partial(quarter_kernel, slots),
        grid=(SOURCES // step_sources,),
        in_specs=quarter_specs(step_sources, half, side, place),
        out_specs=[
            pl.BlockSpec((8, slots), lambda i: (0, i)),
            pl.BlockSpec((8, 16, CODES), lambda i: (0, 0, 0)),
        ],
        out_shape=[
            jax.ShapeDtypeStruct((8, HALF_SLOTS), F32),
            jax.ShapeDtypeStruct((8, 16, CODES), F32),
        ],
        scratch_shapes=[pltpu.VMEM((2, 256, 256), F32)],
        compiler_params=params(56),
        cost_estimate=cost(11e9, 5 * MIB),
    )(rows, picked, ids, targets, book)


def last_sums_kernel(slots, rows_ref, pick_ref, ids_ref, target_ref, s00, s01, s10, count_ref, out_ref, acc_ref):
    step = pl.program_id(0)

    @pl.when(step == 0)
    def _():
        acc_ref[...] = jnp.zeros_like(acc_ref)
        out_ref[:, 16:, :] = jnp.zeros((OWNERS, 8, 128), F32)

    resid = residual(rows_ref, pick_ref, slots)
    flipped = resid.astype(F32).T.astype(BF)
    add_sums(slots, flipped, ids_ref[...] >= 0, target_ref[0], acc_ref)

    @pl.when(step == pl.num_programs(0) - 1)
    def _():
        for m in range(16):
            total = s00[m] + s01[m] if m < 8 else s10[m - 8] + sum_of(acc_ref, m - 8)
            for h in range(2):
                out_ref[2 * m + h, :8, :] = total[8 * h : 8 * h + 8, :128]
                out_ref[2 * m + h, 8:16, :] = total[8 * h : 8 * h + 8, 128:]
                out_ref[2 * m + h, 16:18, :] = count_ref[m]


def last_sums(rows, picked, ids, targets, s00, s01, s10, counts):
    step_sources = 32
    slots = step_sources * HALF
    whole = [pl.BlockSpec((8, 16, CODES), lambda i: (0, 0, 0))] * 3
    return pl.pallas_call(
        functools.partial(last_sums_kernel, slots),
        grid=(SOURCES // step_sources,),
        in_specs=[
            *quarter_specs(step_sources, 1, 1, 0)[:4],
            *whole,
            pl.BlockSpec((16, 2, 128), lambda i: (0, 0, 0)),
        ],
        out_specs=pl.BlockSpec((OWNERS, 24, 128), lambda i: (0, 0, 0)),
        out_shape=jax.ShapeDtypeStruct((OWNERS, 24, 128), F32),
        scratch_shapes=[pltpu.VMEM((2, 256, 256), F32)],
        compiler_params=params(56),
        cost_estimate=cost(2e9, 5 * MIB),
    )(rows, picked, ids, targets, s00, s01, s10, counts)


def last_errors_kernel(slots, rows_ref, pick_ref, ids_ref, target_ref, book_ref, e00, e01, e10, *rest):
    del target_ref
    out_ref = rest[-1]
    resid = residual(rows_ref, pick_ref, slots)
    flipped = resid.astype(F32).T
    last = least_errors(slots, resid, flipped, ids_ref[...] >= 0, book_ref)
    e11 = jnp.concatenate(last, axis=0)
    side = lax.broadcasted_iota(I32, (8, CAP), 1) < HALF
    for at, (lower, upper) in enumerate(((e00[...], e01[...]), (e10[...], e11))):
        for b in range(slots // CAP):
            low = lower[:, b * CAP : (b + 1) * CAP]
            up = upper[:, b * CAP : (b + 1) * CAP]
            even = jnp.where(side, low, pltpu.roll(up, HALF, 1))
            odd = jnp.where(side, pltpu.roll(low, HALF, 1), up)
            out_ref[8 * at : 8 * at + 8, 2 * b * CAP : (2 * b + 1) * CAP] = even
            out_ref[8 * at : 8 * at + 8, (2 * b + 1) * CAP : (2 * b + 2) * CAP] = odd


def last_errors(begin, end, rows, picked, ids, targets, book, e00, e01, e10, before):
    step_sources = 16
    slots = step_sources * HALF
    block = [pl.BlockSpec((8, slots), lambda i: (0, i + begin))] * 3
    earlier = [] if before is None else [before]
    return pl.pallas_call(
        functools.partial(last_errors_kernel, slots),
        grid=(end - begin,),
        in_specs=[
            *quarter_specs(step_sources, 1, 1, 0, begin),
            *block,
            *[pl.BlockSpec(memory_space=pl.ANY) for _ in earlier],
        ],
        out_specs=pl.BlockSpec((16, 2 * slots), lambda i: (0, i + begin)),
        out_shape=jax.ShapeDtypeStruct((16, SLOTS), F32),
        input_output_aliases={} if before is None else {8: 0},
        compiler_params=params(56),
        cost_estimate=cost(1.1e9 * (end - begin), (end - begin) * MIB),
    )(rows, picked, ids, targets, book, e00, e01, e10, *earlier)


def piece_kernel(got_ref, code_ref, out_ref):
    total = jnp.sum(got_ref[...], axis=0)
    codes = code_ref[...]
    low = (codes[:, :128] + total[:8]) / (1.0 + total[16:17])
    high = (codes[:, 128:] + total[8:16]) / (1.0 + total[17:18])
    piece = jnp.concatenate([low, high], axis=1)
    out_ref[...] = jnp.broadcast_to(piece[None], (OWNERS, 8, CODES))


def new_piece(got, codes):
    return pl.pallas_call(
        piece_kernel,
        out_shape=jax.ShapeDtypeStruct((OWNERS, 8, CODES), F32),
        compiler_params=pltpu.CompilerParams(vmem_limit_bytes=56 * MIB),
        cost_estimate=cost(1e6, MIB),
    )(got, codes)


def exchange(x, axes):
    return lax.all_to_all(x, axes, split_axis=0, concat_axis=0, tiled=True)


def per_device(
    embeddings, owner_of_row, list_in_owner, opq_matrix, centroids, codebook, code_targets
):
    every = ("sub", "lists")
    place, start, ids = rank_rows(owner_of_row.reshape(1, ROWS), list_in_owner.reshape(1, ROWS))
    send_a, rest = route(0, start, place, ids, embeddings, opq_matrix)
    rows_a = exchange(send_a.reshape(SOURCES, HALF + ID_ROWS, 128), every)
    send_b, send_c = route(1, start, place, rest, embeddings, opq_matrix)
    book = make_book(codebook)
    targets = code_targets.reshape(16, SOURCES, 2, HALF).transpose(2, 0, 1, 3)
    targets = targets.reshape(2, 16, HALF_SLOTS)
    me = lax.axis_index("lists")
    codes = codebook.astype(F32).reshape(OWNERS, 8, CODES)
    codes = lax.dynamic_slice(codes, (me, 0, 0), (1, 8, CODES))[0]
    send_b, book, targets, codes = lax.optimization_barrier((send_b, book, targets, codes))
    rows_b = exchange(send_b.reshape(SOURCES, CAP, 128), every)
    picked, lower, upper, counts = pick(rows_a, centroids, code_targets)
    counts = counts.reshape(16, 2, 128)
    e00, s00 = quarter(0, 0, 0, rows_a, picked, lower, targets, book)
    send_c, e00, counts = lax.optimization_barrier((send_c, e00, counts))
    rows_c = exchange(send_c.reshape(SOURCES, HALF, 128), every)
    e01, s01 = quarter(0, 1, 0, rows_b, picked, upper, targets, book)
    e10, s10 = quarter(1, 0, 1, rows_b, picked, lower, targets, book)
    rows_c, s01, s10 = lax.optimization_barrier((rows_c, s01, s10))
    pieces = last_sums(rows_c, picked, upper, targets, s00, s01, s10, counts)
    quant_error = last_errors(0, 2, rows_c, picked, upper, targets, book, e00, e01, e10, None)
    got = exchange(pieces, "lists")
    piece, quant_error = lax.optimization_barrier((new_piece(got, codes), quant_error))
    spread = exchange(piece, "lists")
    quant_error = last_errors(
        2, 8, rows_c, picked, upper, targets, book, e00, e01, e10, quant_error
    )
    return quant_error, spread.reshape(16, 16, CODES)


def solution(mesh):
    placed = (
        P(("lists", "sub"), None),
        P(("lists", "sub"), None),
        P(("lists", "sub")),
        P(),
        P("lists", "sub"),
        P("sub", None, None),
        P("sub", "lists"),
    )
    return jax.shard_map(
        per_device,
        mesh=mesh,
        in_specs=placed,
        out_specs=(P("sub", "lists"), P("sub", None, None)),
        check_vma=False,
    )
```

```python
import functools

import jax
import jax.numpy as jnp
from jax import lax
from jax.experimental import pallas as pl
from jax.experimental.pallas import tpu as pltpu
from jax.sharding import PartitionSpec as P

BF = jnp.bfloat16
F32 = jnp.float32
I32 = jnp.int32
I16 = jnp.int16
OWNERS = 32
GROUPS = 4
CAP = 128
ROWS = 2048
WIDTH = 1024
SOURCES = OWNERS * GROUPS
SLOTS = SOURCES * CAP
LISTS = 2048
CODES = 256
MIB = 2**20


def nn(a, b):
    return jnp.dot(a, b, preferred_element_type=F32)


def nt(a, b):
    return lax.dot_general(a, b, (((1,), (1,)), ((), ())), preferred_element_type=F32)


def params(mib):
    return pltpu.CompilerParams(
        vmem_limit_bytes=mib * MIB, dimension_semantics=("arbitrary",)
    )


def cost(flops, bytes_accessed):
    return pl.CostEstimate(
        flops=int(flops), bytes_accessed=int(bytes_accessed), transcendentals=0
    )


ORDERED = ROWS + 16 * OWNERS
ID_ROWS = 8
HALF = CAP // 2
HALF_SLOTS = SOURCES * HALF


def rank_rows(owner, lists):
    owner_hot = (owner == lax.broadcasted_iota(I32, (OWNERS, ROWS), 0)).astype(F32)
    before = (
        lax.broadcasted_iota(I32, (128, 128), 0) < lax.broadcasted_iota(I32, (128, 128), 1)
    ).astype(F32)
    blocks = ROWS // 128
    stacked = jnp.concatenate(
        [owner_hot[:, b * 128 : (b + 1) * 128] for b in range(blocks)], axis=0
    ).astype(BF)
    inside = nn(stacked, before.astype(BF))
    ranks = []
    carry = jnp.zeros((OWNERS, 1), F32)
    for b in range(blocks):
        hot = owner_hot[:, b * 128 : (b + 1) * 128]
        earlier = inside[b * OWNERS : (b + 1) * OWNERS] + carry
        ranks.append(jnp.sum(hot * earlier, axis=0, keepdims=True))
        carry = carry + jnp.sum(hot, axis=1, keepdims=True)
    rank = jnp.concatenate(ranks, axis=1)
    pages = ((carry.astype(I32) + 15) // 16).astype(F32).astype(BF)
    after = before[:OWNERS, :OWNERS].T.astype(BF)
    first = nn(after, jnp.broadcast_to(pages, (OWNERS, 128)))
    begin = jnp.sum(owner_hot * first[:, :1], axis=0, keepdims=True) * 16.0
    place = (begin + rank).astype(I32)
    rank = rank.astype(I32)
    rank_hot = (rank == lax.broadcasted_iota(I32, (CAP, ROWS), 0)).astype(F32).astype(BF)
    high = (lists // 128).astype(F32)
    low = (lists % 128).astype(F32)
    left = jnp.concatenate([owner_hot * high, owner_hot * low, owner_hot], axis=0).astype(BF)
    found = nt(left, rank_hot)
    number = found[:OWNERS] * 128.0 + found[OWNERS : 2 * OWNERS]
    ids = (number + found[2 * OWNERS :] - 1.0).astype(I32)
    return rank, place, first.astype(I32), ids


def matrix_columns(half):
    return [
        pl.BlockSpec((WIDTH, 128), functools.partial(lambda col, i: (0, col), 2 * g + half))
        for g in range(GROUPS)
    ]


def first_route_kernel(parts, step_owners, owner_ref, list_ref, rows_hbm, r0, r1, r2, r3,
                       low_ref, rot_hbm, place_ref, start_ref,
                       slot_ref, ids_ref, rows_ref, rot_ref, in_sem, out_sem):
    step = pl.program_id(0)
    part_rows = ROWS // parts
    count = step_owners * HALF

    def kept():
        return pltpu.make_async_copy(rot_ref, rot_hbm, out_sem)

    @pl.when(step == 0)
    def _():
        copies = []
        for k in range(parts):
            part = pl.ds(k * part_rows, part_rows)
            copies.append(
                pltpu.make_async_copy(rows_hbm.at[part], rows_ref.at[part], in_sem.at[k])
            )
            copies[k].start()
        owner = owner_ref[...]
        rank, place, first, ids = rank_rows(owner, list_ref[...])
        place_ref[...] = place
        start_ref[...] = first
        ids_ref[...] = ids
        slot_ref[...] = jnp.where(rank < HALF, owner * HALF + rank, -1)
        matrix = jnp.concatenate([r[...] for r in (r0, r1, r2, r3)], axis=1)
        for k in range(parts):
            part = pl.ds(k * part_rows, part_rows)
            copies[k].wait()
            rot_ref[part, :] = nn(rows_ref[part, :], matrix).astype(BF)
        kept().start()

    slot = (slot_ref[...] - step * count).astype(I16)
    digit = lax.broadcasted_iota(I32, (count, ROWS), 0).astype(I16)
    hot = jnp.where(slot == digit, jnp.ones((), BF), jnp.zeros((), BF))
    sent = nn(hot, rot_ref[...]).astype(BF)
    line = lax.broadcasted_iota(I32, (ID_ROWS, CAP), 0)
    for j in range(step_owners):
        ids = ids_ref[pl.ds(step * step_owners + j, 1), :]
        high = jnp.where(ids < 0, -1, ids // 128)
        low = ids % 128
        tail = jnp.where(line == 0, high, jnp.where(line == 1, low, 0))
        tail = tail.astype(F32).astype(BF)
        for g in range(GROUPS):
            low_ref[g, j, :HALF, :] = sent[j * HALF : (j + 1) * HALF, g * 128 : (g + 1) * 128]
            low_ref[g, j, HALF:, :] = tail

    @pl.when(step == pl.num_programs(0) - 1)
    def _():
        kept().wait()


def first_route(owner, lists, embeddings, matrix):
    step_owners = 16
    parts = 4
    depth = HALF + ID_ROWS
    return pl.pallas_call(
        functools.partial(first_route_kernel, parts, step_owners),
        grid=(OWNERS // step_owners,),
        in_specs=[
            pl.BlockSpec((1, ROWS), lambda i: (0, 0)),
            pl.BlockSpec((1, ROWS), lambda i: (0, 0)),
            pl.BlockSpec(memory_space=pl.ANY),
            *matrix_columns(0),
        ],
        out_specs=[
            pl.BlockSpec((GROUPS, step_owners, depth, 128), lambda i: (0, i, 0, 0)),
            pl.BlockSpec(memory_space=pl.ANY),
            pl.BlockSpec((1, ROWS), lambda i: (0, 0)),
            pl.BlockSpec((OWNERS, 128), lambda i: (0, 0)),
        ],
        out_shape=[
            jax.ShapeDtypeStruct((GROUPS, OWNERS, depth, 128), BF),
            jax.ShapeDtypeStruct((ROWS, GROUPS * 128), BF),
            jax.ShapeDtypeStruct((1, ROWS), I32),
            jax.ShapeDtypeStruct((OWNERS, 128), I32),
        ],
        scratch_shapes=[
            pltpu.VMEM((1, ROWS), I32),
            pltpu.VMEM((OWNERS, CAP), I32),
            pltpu.VMEM((ROWS, WIDTH), BF),
            pltpu.VMEM((ROWS, GROUPS * 128), BF),
            pltpu.SemaphoreType.DMA((parts,)),
            pltpu.SemaphoreType.DMA,
        ],
        compiler_params=params(60),
        cost_estimate=cost(8e9, 10 * MIB),
    )(owner, lists, embeddings, matrix, matrix, matrix, matrix)


def second_route_kernel(rot_steps, row_steps, step_owners, start_ref, place_ref, rot0_ref, rows_ref,
                        r0, r1, r2, r3, both_ref, high_ref, rot_ref, run_ref):
    step = pl.program_id(0)
    rot_rows = ROWS // rot_steps
    run_rows = ORDERED // row_steps
    wide = GROUPS * 128

    @pl.when(step < rot_steps)
    def _():
        matrix = jnp.concatenate([r[...] for r in (r0, r1, r2, r3)], axis=1)
        at = pl.multiple_of(step * rot_rows, rot_rows)
        rot_ref[pl.ds(at, rot_rows), :] = nn(rows_ref[...], matrix).astype(BF)

    @pl.when(step == 0)
    def _():
        run_ref[ORDERED:, :] = jnp.zeros((CAP, 2 * wide), BF)

    @pl.when(step == rot_steps)
    def _():
        one = jnp.ones((), BF)
        zero = jnp.zeros((), BF)
        digit = lax.broadcasted_iota(I32, (run_rows, ROWS), 0).astype(I16)
        for k in range(row_steps):
            place = (place_ref[...] - k * run_rows).astype(I16)
            hot = jnp.where(place == digit, one, zero)
            part = slice(k * run_rows, (k + 1) * run_rows)
            run_ref[part, :wide] = nn(hot, rot0_ref[...]).astype(BF)
            run_ref[part, wide:] = nn(hot, rot_ref[...]).astype(BF)

    @pl.when(step >= rot_steps)
    def _():
        for j in range(step_owners):
            owner = (step - rot_steps) * step_owners + j
            begin = pl.multiple_of(start_ref[owner, 0] * 16, 16)
            run = run_ref[pl.ds(begin, CAP), :]
            for g in range(GROUPS):
                mine = slice(g * 128, (g + 1) * 128)
                both_ref[g, j, :HALF, :] = run[HALF:, mine]
                both_ref[g, j, HALF:, :] = run[:HALF, wide + g * 128 : wide + (g + 1) * 128]
                high_ref[g, j] = run[HALF:, wide + g * 128 : wide + (g + 1) * 128]


def second_route(start, place, rot0, embeddings, matrix):
    step_owners = 8
    rot_steps = 2
    row_steps = 5

    def by_owner(i):
        return (0, jnp.maximum(i - rot_steps, 0), 0, 0)

    return pl.pallas_call(
        functools.partial(second_route_kernel, rot_steps, row_steps, step_owners),
        grid=(rot_steps + OWNERS // step_owners,),
        in_specs=[
            pl.BlockSpec(memory_space=pltpu.SMEM),
            pl.BlockSpec((1, ROWS), lambda i: (0, 0)),
            pl.BlockSpec((ROWS, GROUPS * 128), lambda i: (0, 0)),
            pl.BlockSpec((ROWS // rot_steps, WIDTH), lambda i: (jnp.minimum(i, rot_steps - 1), 0)),
            *matrix_columns(1),
        ],
        out_specs=[pl.BlockSpec((GROUPS, step_owners, d, 128), by_owner) for d in (CAP, HALF)],
        out_shape=[jax.ShapeDtypeStruct((GROUPS, OWNERS, d, 128), BF) for d in (CAP, HALF)],
        scratch_shapes=[
            pltpu.VMEM((ROWS, GROUPS * 128), BF),
            pltpu.VMEM((ORDERED + CAP, 2 * GROUPS * 128), BF),
        ],
        compiler_params=params(60),
        cost_estimate=cost(13e9, 12 * MIB),
    )(start, place, rot0, embeddings, matrix, matrix, matrix, matrix)


def pick_kernel(step_sources, tail_ref, centroid_ref, target_ref, out_ref, lower_ref, upper_ref, count_ref, acc_ref):
    step = pl.program_id(0)

    @pl.when(step == 0)
    def _():
        acc_ref[...] = jnp.zeros_like(acc_ref)

    slots = step_sources * CAP
    one = jnp.ones((), BF)
    zero = jnp.zeros((), BF)
    lane = lax.broadcasted_iota(I32, (CAP, 128), 1).astype(I16)
    numbers = []
    hots = []
    for j in range(step_sources):
        tail = tail_ref[j, HALF:, :].astype(F32)
        number = tail[0:1, :] * 128.0 + tail[1:2, :]
        numbers.append(number)
        column = jnp.broadcast_to(number, (128, CAP)).T.astype(I32).astype(I16)
        hots.append(
            jnp.concatenate(
                [
                    jnp.where(column == lane + jnp.int16(128 * b), one, zero)
                    for b in range(LISTS // 128)
                ],
                axis=1,
            )
        )
    found = nn(jnp.concatenate(hots, axis=0), centroid_ref[...]).astype(BF)
    out_ref[...] = found.reshape(step_sources, CAP, 256)
    side = lax.broadcasted_iota(I32, (1, CAP), 1) < HALF
    lower = []
    upper = []
    for j in range(0, step_sources, 2):
        even, odd = numbers[j], numbers[j + 1]
        lower.append(jnp.where(side, even, pltpu.roll(odd, HALF, 1)))
        upper.append(jnp.where(side, pltpu.roll(even, HALF, 1), odd))
    lower_ref[...] = jnp.concatenate(lower, axis=1)
    upper_ref[...] = jnp.concatenate(upper, axis=1)

    live = jnp.concatenate(numbers, axis=1) >= 0
    target = jnp.where(live, target_ref[...], -1)
    high = jnp.where(live, target // 16, -1).astype(I16)
    low = (target % 16).astype(I16)
    digit = lax.broadcasted_iota(I32, (16, slots), 0).astype(I16)
    left = []
    right = []
    for m in range(16):
        left.append(jnp.where(high[m : m + 1] == digit, one, zero))
        right.append(jnp.where(low[m : m + 1] == digit, one, zero))
    acc_ref[...] += nt(jnp.concatenate(left, axis=0), jnp.concatenate(right, axis=0))

    @pl.when(step == pl.num_programs(0) - 1)
    def _():
        for m in range(16):
            block = acc_ref[m * 16 : (m + 1) * 16, m * 16 : (m + 1) * 16]
            count_ref[m] = block


def pick(rows0, centroids, targets):
    step_sources = 16
    slots = step_sources * CAP
    return pl.pallas_call(
        functools.partial(pick_kernel, step_sources),
        grid=(SOURCES // step_sources,),
        in_specs=[
            pl.BlockSpec((step_sources, HALF + ID_ROWS, CAP), lambda i: (i, 0, 0)),
            pl.BlockSpec((LISTS, 256), lambda i: (0, 0)),
            pl.BlockSpec((16, slots), lambda i: (0, i)),
        ],
        out_specs=[
            pl.BlockSpec((step_sources, CAP, 256), lambda i: (i, 0, 0)),
            pl.BlockSpec((1, slots // 2), lambda i: (0, i)),
            pl.BlockSpec((1, slots // 2), lambda i: (0, i)),
            pl.BlockSpec((16, 16, 16), lambda i: (0, 0, 0)),
        ],
        out_shape=[
            jax.ShapeDtypeStruct((SOURCES, CAP, 256), BF),
            jax.ShapeDtypeStruct((1, HALF_SLOTS), F32),
            jax.ShapeDtypeStruct((1, HALF_SLOTS), F32),
            jax.ShapeDtypeStruct((16, 16, 16), F32),
        ],
        scratch_shapes=[pltpu.VMEM((256, 256), F32)],
        compiler_params=params(60),
        cost_estimate=cost(20e9, 12 * MIB),
    )(rows0, centroids, targets)


def book_kernel(code_ref, out_ref):
    codes = code_ref[...].astype(F32).T
    lane = lax.broadcasted_iota(I32, (CODES, 128), 1)
    for m in range(8):
        mine = jnp.where(lane // 16 == m, codes, 0.0)
        square = jnp.sum(mine * mine, axis=1, keepdims=True)
        high = square.astype(BF).astype(F32)
        middle = (square - high).astype(BF).astype(F32)
        low = square - high - middle
        tail = jnp.where(
            lane == 0, high, jnp.where(lane == 1, middle, jnp.where(lane == 2, low, 0.0))
        )
        out_ref[m * CODES : (m + 1) * CODES, :128] = (-2.0 * mine).astype(BF)
        out_ref[m * CODES : (m + 1) * CODES, 128:] = tail.astype(BF)


def make_book(codebook):
    return pl.pallas_call(
        book_kernel,
        grid=(2,),
        in_specs=[pl.BlockSpec((128, CODES), lambda i: (i, 0))],
        out_specs=pl.BlockSpec((8 * CODES, 256), lambda i: (i, 0)),
        out_shape=jax.ShapeDtypeStruct((16 * CODES, 256), BF),
        compiler_params=params(60),
        cost_estimate=cost(1e9, 3 * MIB),
    )(codebook.reshape(256, CODES))


def residual(rows_ref, pick_ref, slots):
    rows = rows_ref[...].reshape(slots, 128).astype(F32)
    centre = pick_ref[...].reshape(slots, 128).astype(F32)
    return (rows - centre).astype(BF)


def add_sums(slots, flipped, live, target, acc_ref):
    high = jnp.where(live, target // 64, -1).astype(I16)
    low = (target % 64).astype(I16)
    digit = lax.broadcasted_iota(I32, (64, slots), 0).astype(I16)
    one = jnp.ones((), BF)
    zero = jnp.zeros((), BF)
    for t in range(2):
        left = []
        right = []
        for m in range(4 * t, 4 * t + 4):
            mine = flipped[m * 16 : (m + 1) * 16]
            row = jnp.broadcast_to(high[m : m + 1], (16, slots))
            for h in range(4):
                left.append(jnp.where(row == jnp.int16(h), mine, zero))
            right.append(jnp.where(low[m : m + 1] == digit, one, zero))
        acc_ref[t] += nt(jnp.concatenate(left, axis=0), jnp.concatenate(right, axis=0))


def sum_of(acc_ref, m):
    base = (m % 4) * 64
    part = acc_ref[m // 4][:, base : base + 64]
    return jnp.concatenate([part[base + h * 16 : base + (h + 1) * 16] for h in range(4)], axis=1)


def least_errors(slots, resid, flipped, live, book_ref):
    wide = jnp.concatenate([resid, jnp.ones((slots, 128), BF)], axis=1)
    lines = []
    for m in range(8):
        mine = flipped[m * 16 : (m + 1) * 16]
        row_sq = jnp.sum(mine * mine, axis=0, keepdims=True)
        dist = nt(book_ref[m * CODES : (m + 1) * CODES], wide)
        least = jnp.min(dist, axis=0, keepdims=True)
        lines.append(jnp.where(live, row_sq + least, 0.0))
    return lines


def quarter_kernel(slots, rows_ref, pick_ref, ids_ref, target_ref, book_ref, error_ref, sum_ref, acc_ref):
    step = pl.program_id(0)

    @pl.when(step == 0)
    def _():
        acc_ref[...] = jnp.zeros_like(acc_ref)

    resid = residual(rows_ref, pick_ref, slots)
    flipped = resid.astype(F32).T
    live = ids_ref[...] >= 0
    add_sums(slots, flipped.astype(BF), live, target_ref[0], acc_ref)
    for m, line in enumerate(least_errors(slots, resid, flipped, live, book_ref)):
        error_ref[m : m + 1, :] = line

    @pl.when(step == pl.num_programs(0) - 1)
    def _():
        for m in range(8):
            sum_ref[m] = sum_of(acc_ref, m)


def quarter_specs(step_sources, half, side, place, begin=0):
    slots = step_sources * HALF
    return [
        pl.BlockSpec((step_sources, HALF, 128), lambda i: (i + begin, place, 0)),
        pl.BlockSpec((step_sources, HALF, 128), lambda i: (i + begin, side, half)),
        pl.BlockSpec((1, slots), lambda i: (0, i + begin)),
        pl.BlockSpec((1, 8, slots), lambda i: (side, half, i + begin)),
        pl.BlockSpec((8 * CODES, 256), lambda i: (half, 0)),
    ]


def quarter(half, side, place, rows, picked, ids, targets, book):
    step_sources = 32
    slots = step_sources * HALF
    return pl.pallas_call(
        functools.partial(quarter_kernel, slots),
        grid=(SOURCES // step_sources,),
        in_specs=quarter_specs(step_sources, half, side, place),
        out_specs=[
            pl.BlockSpec((8, slots), lambda i: (0, i)),
            pl.BlockSpec((8, 16, CODES), lambda i: (0, 0, 0)),
        ],
        out_shape=[
            jax.ShapeDtypeStruct((8, HALF_SLOTS), F32),
            jax.ShapeDtypeStruct((8, 16, CODES), F32),
        ],
        scratch_shapes=[pltpu.VMEM((2, 256, 256), F32)],
        compiler_params=params(60),
        cost_estimate=cost(11e9, 5 * MIB),
    )(rows, picked, ids, targets, book)


def last_sums_kernel(slots, rows_ref, pick_ref, ids_ref, target_ref, s00, s01, s10, count_ref, out_ref, acc_ref):
    step = pl.program_id(0)

    @pl.when(step == 0)
    def _():
        acc_ref[...] = jnp.zeros_like(acc_ref)
        out_ref[:, 16:, :] = jnp.zeros((OWNERS, 8, 128), F32)

    resid = residual(rows_ref, pick_ref, slots)
    flipped = resid.astype(F32).T.astype(BF)
    add_sums(slots, flipped, ids_ref[...] >= 0, target_ref[0], acc_ref)

    @pl.when(step == pl.num_programs(0) - 1)
    def _():
        for m in range(16):
            total = s00[m] + s01[m] if m < 8 else s10[m - 8] + sum_of(acc_ref, m - 8)
            for h in range(2):
                out_ref[2 * m + h, :8, :] = total[8 * h : 8 * h + 8, :128]
                out_ref[2 * m + h, 8:16, :] = total[8 * h : 8 * h + 8, 128:]
                out_ref[2 * m + h, 16:18, :] = count_ref[m]


def last_sums(rows, picked, ids, targets, s00, s01, s10, counts):
    step_sources = 64
    slots = step_sources * HALF
    whole = [pl.BlockSpec((8, 16, CODES), lambda i: (0, 0, 0))] * 3
    return pl.pallas_call(
        functools.partial(last_sums_kernel, slots),
        grid=(SOURCES // step_sources,),
        in_specs=[
            *quarter_specs(step_sources, 1, 1, 0)[:4],
            *whole,
            pl.BlockSpec((16, 2, 128), lambda i: (0, 0, 0)),
        ],
        out_specs=pl.BlockSpec((OWNERS, 24, 128), lambda i: (0, 0, 0)),
        out_shape=jax.ShapeDtypeStruct((OWNERS, 24, 128), F32),
        scratch_shapes=[pltpu.VMEM((2, 256, 256), F32)],
        compiler_params=params(60),
        cost_estimate=cost(2e9, 5 * MIB),
    )(rows, picked, ids, targets, s00, s01, s10, counts)


def last_errors_kernel(slots, rows_ref, pick_ref, ids_ref, target_ref, book_ref, e00, e01, e10, *rest):
    del target_ref
    out_ref = rest[-1]
    resid = residual(rows_ref, pick_ref, slots)
    flipped = resid.astype(F32).T
    last = least_errors(slots, resid, flipped, ids_ref[...] >= 0, book_ref)
    e11 = jnp.concatenate(last, axis=0)
    side = lax.broadcasted_iota(I32, (8, CAP), 1) < HALF
    for at, (lower, upper) in enumerate(((e00[...], e01[...]), (e10[...], e11))):
        for b in range(slots // CAP):
            low = lower[:, b * CAP : (b + 1) * CAP]
            up = upper[:, b * CAP : (b + 1) * CAP]
            even = jnp.where(side, low, pltpu.roll(up, HALF, 1))
            odd = jnp.where(side, pltpu.roll(low, HALF, 1), up)
            out_ref[8 * at : 8 * at + 8, 2 * b * CAP : (2 * b + 1) * CAP] = even
            out_ref[8 * at : 8 * at + 8, (2 * b + 1) * CAP : (2 * b + 2) * CAP] = odd


def last_errors(begin, end, rows, picked, ids, targets, book, e00, e01, e10, before):
    step_sources = 32
    slots = step_sources * HALF
    block = [pl.BlockSpec((8, slots), lambda i: (0, i + begin))] * 3
    earlier = [] if before is None else [before]
    return pl.pallas_call(
        functools.partial(last_errors_kernel, slots),
        grid=(end - begin,),
        in_specs=[
            *quarter_specs(step_sources, 1, 1, 0, begin),
            *block,
            *[pl.BlockSpec(memory_space=pl.ANY) for _ in earlier],
        ],
        out_specs=pl.BlockSpec((16, 2 * slots), lambda i: (0, i + begin)),
        out_shape=jax.ShapeDtypeStruct((16, SLOTS), F32),
        input_output_aliases={} if before is None else {8: 0},
        compiler_params=params(60),
        cost_estimate=cost(2.2e9 * (end - begin), (end - begin) * 2 * MIB),
    )(rows, picked, ids, targets, book, e00, e01, e10, *earlier)


def new_piece(got, codes):
    total = jnp.sum(got, axis=0)
    low = (codes[:, :128] + total[:8]) / (1.0 + total[16:17])
    high = (codes[:, 128:] + total[8:16]) / (1.0 + total[17:18])
    piece = jnp.concatenate([low, high], axis=1)
    return jnp.broadcast_to(piece[None], (OWNERS, 8, CODES))


def exchange(x, axes):
    return lax.all_to_all(x, axes, split_axis=0, concat_axis=0, tiled=True)


def per_device(
    embeddings, owner_of_row, list_in_owner, opq_matrix, centroids, codebook, code_targets
):
    every = ("sub", "lists")
    owner = owner_of_row.reshape(1, ROWS)
    lists = list_in_owner.reshape(1, ROWS)
    send_a, rot0, place, start = first_route(owner, lists, embeddings, opq_matrix)
    rows_a = exchange(send_a.reshape(SOURCES, HALF + ID_ROWS, 128), every)
    send_b, send_c = second_route(start, place, rot0, embeddings, opq_matrix)
    book = make_book(codebook)
    targets = code_targets.reshape(16, SOURCES, 2, HALF).transpose(2, 0, 1, 3)
    targets = targets.reshape(2, 16, HALF_SLOTS)
    me = lax.axis_index("lists")
    codes = codebook.astype(F32).reshape(OWNERS, 8, CODES)
    codes = lax.dynamic_slice(codes, (me, 0, 0), (1, 8, CODES))[0]
    send_b, book, targets, codes = lax.optimization_barrier((send_b, book, targets, codes))
    rows_b = exchange(send_b.reshape(SOURCES, CAP, 128), every)
    picked, lower, upper, counts = pick(rows_a, centroids, code_targets)
    counts = counts.reshape(16, 2, 128)
    e00, s00 = quarter(0, 0, 0, rows_a, picked, lower, targets, book)
    send_c, e00, counts = lax.optimization_barrier((send_c, e00, counts))
    rows_c = exchange(send_c.reshape(SOURCES, HALF, 128), every)
    e01, s01 = quarter(0, 1, 0, rows_b, picked, upper, targets, book)
    e10, s10 = quarter(1, 0, 1, rows_b, picked, lower, targets, book)
    rows_c, s01, s10 = lax.optimization_barrier((rows_c, s01, s10))
    pieces = last_sums(rows_c, picked, upper, targets, s00, s01, s10, counts)
    quant_error = last_errors(0, 2, rows_c, picked, upper, targets, book, e00, e01, e10, None)
    got = exchange(pieces, "lists")
    piece, quant_error = lax.optimization_barrier((new_piece(got, codes), quant_error))
    spread = exchange(piece, "lists")
    quant_error = last_errors(
        2, 4, rows_c, picked, upper, targets, book, e00, e01, e10, quant_error
    )
    return quant_error, spread.reshape(16, 16, CODES)


def solution(mesh):
    placed = (
        P(("lists", "sub"), None),
        P(("lists", "sub"), None),
        P(("lists", "sub")),
        P(),
        P("lists", "sub"),
        P("sub", None, None),
        P("sub", "lists"),
    )
    return jax.shard_map(
        per_device,
        mesh=mesh,
        in_specs=placed,
        out_specs=(P("sub", "lists"), P("sub", None, None)),
        check_vma=False,
    )
```

```python
import functools

import jax
import jax.numpy as jnp
from jax import lax
from jax.experimental import pallas as pl
from jax.experimental.pallas import tpu as pltpu
from jax.sharding import PartitionSpec as P

BF = jnp.bfloat16
F32 = jnp.float32
I32 = jnp.int32
I16 = jnp.int16
OWNERS = 32
GROUPS = 4
CAP = 128
ROWS = 2048
WIDTH = 1024
SOURCES = OWNERS * GROUPS
SLOTS = SOURCES * CAP
LISTS = 2048
CODES = 256
MIB = 2**20


def nn(a, b):
    return jnp.dot(a, b, preferred_element_type=F32)


def nt(a, b):
    return lax.dot_general(a, b, (((1,), (1,)), ((), ())), preferred_element_type=F32)


def params(mib):
    return pltpu.CompilerParams(
        vmem_limit_bytes=mib * MIB, dimension_semantics=("arbitrary",)
    )


def cost(flops, bytes_accessed):
    return pl.CostEstimate(
        flops=int(flops), bytes_accessed=int(bytes_accessed), transcendentals=0
    )


ORDERED = ROWS + 16 * OWNERS
ID_ROWS = 8


def rank_rows(owner, lists):
    owner_hot = (owner == lax.broadcasted_iota(I32, (OWNERS, ROWS), 0)).astype(F32)
    before = (
        lax.broadcasted_iota(I32, (128, 128), 0) < lax.broadcasted_iota(I32, (128, 128), 1)
    ).astype(F32)
    blocks = ROWS // 128
    stacked = jnp.concatenate(
        [owner_hot[:, b * 128 : (b + 1) * 128] for b in range(blocks)], axis=0
    ).astype(BF)
    inside = nn(stacked, before.astype(BF))
    ranks = []
    carry = jnp.zeros((OWNERS, 1), F32)
    for b in range(blocks):
        hot = owner_hot[:, b * 128 : (b + 1) * 128]
        earlier = inside[b * OWNERS : (b + 1) * OWNERS] + carry
        ranks.append(jnp.sum(hot * earlier, axis=0, keepdims=True))
        carry = carry + jnp.sum(hot, axis=1, keepdims=True)
    rank = jnp.concatenate(ranks, axis=1)
    pages = ((carry.astype(I32) + 15) // 16).astype(F32).astype(BF)
    after = before[:OWNERS, :OWNERS].T.astype(BF)
    first = nn(after, jnp.broadcast_to(pages, (OWNERS, 128)))
    begin = jnp.sum(owner_hot * first[:, :1], axis=0, keepdims=True) * 16.0
    place = (begin + rank).astype(I32)
    rank = rank.astype(I32)
    rank_hot = (rank == lax.broadcasted_iota(I32, (CAP, ROWS), 0)).astype(F32).astype(BF)
    high = (lists // 128).astype(F32)
    low = (lists % 128).astype(F32)
    left = jnp.concatenate([owner_hot * high, owner_hot * low, owner_hot], axis=0).astype(BF)
    found = nt(left, rank_hot)
    number = found[:OWNERS] * 128.0 + found[OWNERS : 2 * OWNERS]
    ids = (number + found[2 * OWNERS :] - 1.0).astype(I32)
    return place, first.astype(I32), ids


def matrix_columns(half):
    return [
        pl.BlockSpec((WIDTH, 128), functools.partial(lambda col, i: (0, col), 2 * g + half))
        for g in range(GROUPS)
    ]


def order_rows(place, rot_ref, run_ref, row_steps):
    run_rows = ORDERED // row_steps
    one = jnp.ones((), BF)
    zero = jnp.zeros((), BF)
    digit = lax.broadcasted_iota(I32, (run_rows, ROWS), 0).astype(I16)
    for k in range(row_steps):
        hot = jnp.where((place - k * run_rows).astype(I16) == digit, one, zero)
        run_ref[k * run_rows : (k + 1) * run_rows, :] = nn(hot, rot_ref[...]).astype(BF)
    run_ref[ORDERED:, :] = jnp.zeros((CAP, GROUPS * 128), BF)


def route_kernel(half, parts, row_steps, step_owners, *refs):
    if half == 0:
        owner_ref, list_ref, rows_hbm, r0, r1, r2, r3, out_ref, place_ref, first_ref = refs[:10]
        start_ref, ids_ref, rows_ref, rot_ref, run_ref, in_sem, start_sem = refs[10:]
    else:
        start_ref, place_ref, rows_hbm, r0, r1, r2, r3, out_ref = refs[:8]
        rows_ref, rot_ref, run_ref, in_sem = refs[8:]
    step = pl.program_id(0)
    part_rows = ROWS // parts

    @pl.when(step == 0)
    def _():
        copies = []
        for k in range(parts):
            part = pl.ds(k * part_rows, part_rows)
            copies.append(
                pltpu.make_async_copy(rows_hbm.at[part], rows_ref.at[part], in_sem.at[k])
            )
            copies[k].start()
        if half == 0:
            place, first, ids = rank_rows(owner_ref[...], list_ref[...])
            place_ref[...] = place
            first_ref[...] = first
            ids_ref[...] = ids
            starts = pltpu.make_async_copy(first_ref, start_ref, start_sem)
            starts.start()
        matrix = jnp.concatenate([r[...] for r in (r0, r1, r2, r3)], axis=1)
        for k in range(parts):
            part = pl.ds(k * part_rows, part_rows)
            copies[k].wait()
            rot_ref[part, :] = nn(rows_ref[part, :], matrix).astype(BF)
        order_rows(place_ref[...], rot_ref, run_ref, row_steps)
        if half == 0:
            starts.wait()

    line = lax.broadcasted_iota(I32, (ID_ROWS, CAP), 0)
    for j in range(step_owners):
        owner = step * step_owners + j
        begin = pl.multiple_of(start_ref[owner, 0] * 16, 16)
        run = run_ref[pl.ds(begin, CAP), :]
        for g in range(GROUPS):
            out_ref[g, j, :CAP, :] = run[:, g * 128 : (g + 1) * 128]
        if half == 0:
            ids = ids_ref[pl.ds(owner, 1), :]
            high = jnp.where(ids < 0, -1, ids // 128)
            low = ids % 128
            tail = jnp.where(line == 0, high, jnp.where(line == 1, low, 0))
            tail = tail.astype(F32).astype(BF)
            for g in range(GROUPS):
                out_ref[g, j, CAP:, :] = tail


def route(half, first_arg, second_arg, embeddings, matrix):
    step_owners = 8
    parts = 4
    row_steps = 5
    depth = CAP + (ID_ROWS if half == 0 else 0)
    line = pl.BlockSpec((1, ROWS), lambda i: (0, 0))
    out_specs = [pl.BlockSpec((GROUPS, step_owners, depth, 128), lambda i: (0, i, 0, 0))]
    out_shape = [jax.ShapeDtypeStruct((GROUPS, OWNERS, depth, 128), BF)]
    scratch = [
        pltpu.VMEM((ROWS, WIDTH), BF),
        pltpu.VMEM((ROWS, GROUPS * 128), BF),
        pltpu.VMEM((ORDERED + CAP, GROUPS * 128), BF),
        pltpu.SemaphoreType.DMA((parts,)),
    ]
    if half == 0:
        inputs = [line, line]
        out_specs += [line, pl.BlockSpec((OWNERS, 128), lambda i: (0, 0))]
        out_shape += [
            jax.ShapeDtypeStruct((1, ROWS), I32),
            jax.ShapeDtypeStruct((OWNERS, 128), I32),
        ]
        scratch = [
            pltpu.SMEM((OWNERS, 128), I32),
            pltpu.VMEM((OWNERS, CAP), I32),
            *scratch,
            pltpu.SemaphoreType.DMA,
        ]
    else:
        inputs = [pl.BlockSpec(memory_space=pltpu.SMEM), line]
    return pl.pallas_call(
        functools.partial(route_kernel, half, parts, row_steps, step_owners),
        grid=(OWNERS // step_owners,),
        in_specs=[*inputs, pl.BlockSpec(memory_space=pl.ANY), *matrix_columns(half)],
        out_specs=out_specs,
        out_shape=out_shape,
        scratch_shapes=scratch,
        compiler_params=params(60),
        cost_estimate=cost(8e9, 10 * MIB),
    )(first_arg, second_arg, embeddings, matrix, matrix, matrix, matrix)


def pick_kernel(step_sources, tail_ref, centroid_ref, out_ref, ids_ref):
    one = jnp.ones((), BF)
    zero = jnp.zeros((), BF)
    lane = lax.broadcasted_iota(I32, (CAP, 128), 1).astype(I16)
    numbers = []
    hots = []
    for j in range(step_sources):
        tail = tail_ref[j, CAP:, :].astype(F32)
        number = tail[0:1, :] * 128.0 + tail[1:2, :]
        numbers.append(number)
        column = jnp.broadcast_to(number, (128, CAP)).T.astype(I32).astype(I16)
        hots.append(
            jnp.concatenate(
                [
                    jnp.where(column == lane + jnp.int16(128 * b), one, zero)
                    for b in range(LISTS // 128)
                ],
                axis=1,
            )
        )
    found = nn(jnp.concatenate(hots, axis=0), centroid_ref[...]).astype(BF)
    out_ref[...] = found.reshape(step_sources, CAP, 256)
    ids_ref[...] = jnp.concatenate(numbers, axis=1)


def pick(rows0, centroids):
    step_sources = 16
    slots = step_sources * CAP
    return pl.pallas_call(
        functools.partial(pick_kernel, step_sources),
        grid=(SOURCES // step_sources,),
        in_specs=[
            pl.BlockSpec((step_sources, CAP + ID_ROWS, CAP), lambda i: (i, 0, 0)),
            pl.BlockSpec((LISTS, 256), lambda i: (0, 0)),
        ],
        out_specs=[
            pl.BlockSpec((step_sources, CAP, 256), lambda i: (i, 0, 0)),
            pl.BlockSpec((1, slots), lambda i: (0, i)),
        ],
        out_shape=[
            jax.ShapeDtypeStruct((SOURCES, CAP, 256), BF),
            jax.ShapeDtypeStruct((1, SLOTS), F32),
        ],
        compiler_params=params(60),
        cost_estimate=cost(18e9, 14 * MIB),
    )(rows0, centroids)


def book_kernel(code_ref, out_ref):
    codes = code_ref[...].astype(F32).T
    lane = lax.broadcasted_iota(I32, (CODES, 128), 1)
    for m in range(8):
        mine = jnp.where(lane // 16 == m, codes, 0.0)
        square = jnp.sum(mine * mine, axis=1, keepdims=True)
        high = square.astype(BF).astype(F32)
        middle = (square - high).astype(BF).astype(F32)
        low = square - high - middle
        tail = jnp.where(
            lane == 0, high, jnp.where(lane == 1, middle, jnp.where(lane == 2, low, 0.0))
        )
        out_ref[m * CODES : (m + 1) * CODES, :128] = (-2.0 * mine).astype(BF)
        out_ref[m * CODES : (m + 1) * CODES, 128:] = tail.astype(BF)


def make_book(codebook):
    return pl.pallas_call(
        book_kernel,
        grid=(2,),
        in_specs=[pl.BlockSpec((128, CODES), lambda i: (i, 0))],
        out_specs=pl.BlockSpec((8 * CODES, 256), lambda i: (i, 0)),
        out_shape=jax.ShapeDtypeStruct((16 * CODES, 256), BF),
        compiler_params=params(60),
        cost_estimate=cost(1e9, 3 * MIB),
    )(codebook.reshape(256, CODES))


def residual(rows_ref, pick_ref, slots):
    rows = rows_ref[...].reshape(slots, 128).astype(F32)
    centre = pick_ref[...].reshape(slots, 128).astype(F32)
    return (rows - centre).astype(BF)


def add_sums(slots, flipped, live, target, acc_ref):
    high = jnp.where(live, target // 64, -1).astype(I16)
    low = (target % 64).astype(I16)
    digit = lax.broadcasted_iota(I32, (64, slots), 0).astype(I16)
    line = lax.broadcasted_iota(I32, (16, slots), 0)
    nth = (line // 4).astype(I16)
    quarter = (line % 4).astype(I16)
    one = jnp.ones((), BF)
    zero = jnp.zeros((), BF)
    for t in range(2):
        left = []
        right = []
        mixed = jnp.zeros((16, slots), I16)
        for m in range(4 * t, 4 * t + 4):
            mine = flipped[m * 16 : (m + 1) * 16]
            row = jnp.broadcast_to(high[m : m + 1], (16, slots))
            mixed = jnp.where(nth == jnp.int16(m % 4), row, mixed)
            for h in range(4):
                left.append(jnp.where(row == jnp.int16(h), mine, zero))
            right.append(jnp.where(low[m : m + 1] == digit, one, zero))
        left.append(jnp.where(mixed == quarter, one, zero))
        acc_ref[t] += nt(jnp.concatenate(left, axis=0), jnp.concatenate(right, axis=0))


def sum_of(acc_ref, m):
    base = (m % 4) * 64
    part = acc_ref[m // 4][:, base : base + 64]
    return jnp.concatenate([part[base + h * 16 : base + (h + 1) * 16] for h in range(4)], axis=1)


def count_of(acc_ref, m):
    base = (m % 4) * 64
    part = acc_ref[m // 4][256:, base : base + 64]
    at = (m % 4) * 4
    return jnp.concatenate([part[at + h : at + h + 1] for h in range(4)], axis=1)


def least_errors(slots, resid, flipped, live, book_ref):
    wide = jnp.concatenate([resid, jnp.ones((slots, 128), BF)], axis=1)
    lines = []
    for m in range(8):
        mine = flipped[m * 16 : (m + 1) * 16]
        row_sq = jnp.sum(mine * mine, axis=0, keepdims=True)
        dist = nt(book_ref[m * CODES : (m + 1) * CODES], wide)
        least = jnp.min(dist, axis=0, keepdims=True)
        lines.append(jnp.where(live, row_sq + least, 0.0))
    return lines


def half_specs(step_sources, half, begin=0):
    slots = step_sources * CAP
    return [
        pl.BlockSpec((step_sources, CAP, 128), lambda i: (i + begin, 0, 0)),
        pl.BlockSpec((step_sources, CAP, 128), lambda i: (i + begin, 0, half)),
        pl.BlockSpec((1, slots), lambda i: (0, i + begin)),
        pl.BlockSpec((8, slots), lambda i: (half, i + begin)),
        pl.BlockSpec((8 * CODES, 256), lambda i: (half, 0)),
    ]


def first_half_kernel(slots, rows_ref, pick_ref, ids_ref, target_ref, book_ref,
                      error_ref, sum_ref, count_ref, acc_ref):
    step = pl.program_id(0)

    @pl.when(step == 0)
    def _():
        acc_ref[...] = jnp.zeros_like(acc_ref)

    resid = residual(rows_ref, pick_ref, slots)
    flipped = resid.astype(F32).T
    live = ids_ref[...] >= 0
    add_sums(slots, flipped.astype(BF), live, target_ref[...], acc_ref)
    for m, line in enumerate(least_errors(slots, resid, flipped, live, book_ref)):
        error_ref[m : m + 1, :] = line

    @pl.when(step == pl.num_programs(0) - 1)
    def _():
        for m in range(8):
            sum_ref[m] = sum_of(acc_ref, m)
            count_ref[m : m + 1, :] = count_of(acc_ref, m)


def first_half(rows, picked, ids, targets, book):
    step_sources = 32
    slots = step_sources * CAP
    return pl.pallas_call(
        functools.partial(first_half_kernel, slots),
        grid=(SOURCES // step_sources,),
        in_specs=half_specs(step_sources, 0),
        out_specs=[
            pl.BlockSpec((8, slots), lambda i: (0, i)),
            pl.BlockSpec((8, 16, CODES), lambda i: (0, 0, 0)),
            pl.BlockSpec((8, CODES), lambda i: (0, 0)),
        ],
        out_shape=[
            jax.ShapeDtypeStruct((16, SLOTS), F32),
            jax.ShapeDtypeStruct((8, 16, CODES), F32),
            jax.ShapeDtypeStruct((8, CODES), F32),
        ],
        scratch_shapes=[pltpu.VMEM((2, 272, 256), F32)],
        compiler_params=params(60),
        cost_estimate=cost(22e9, 10 * MIB),
    )(rows, picked, ids, targets, book)


def last_sums_kernel(slots, rows_ref, pick_ref, ids_ref, target_ref, sum_ref, count_ref, out_ref, acc_ref):
    step = pl.program_id(0)

    @pl.when(step == 0)
    def _():
        acc_ref[...] = jnp.zeros_like(acc_ref)
        out_ref[:, 16:, :] = jnp.zeros((OWNERS, 8, 128), F32)

    resid = residual(rows_ref, pick_ref, slots)
    flipped = resid.astype(F32).T.astype(BF)
    add_sums(slots, flipped, ids_ref[...] >= 0, target_ref[...], acc_ref)

    @pl.when(step == pl.num_programs(0) - 1)
    def _():
        for m in range(16):
            total = sum_ref[m] if m < 8 else sum_of(acc_ref, m - 8)
            count = count_ref[m : m + 1, :] if m < 8 else count_of(acc_ref, m - 8)
            for h in range(2):
                out_ref[2 * m + h, :8, :] = total[8 * h : 8 * h + 8, :128]
                out_ref[2 * m + h, 8:16, :] = total[8 * h : 8 * h + 8, 128:]
                out_ref[2 * m + h, 16:17, :] = count[:, :128]
                out_ref[2 * m + h, 17:18, :] = count[:, 128:]


def last_sums(rows, picked, ids, targets, sums, counts):
    step_sources = 32
    slots = step_sources * CAP
    return pl.pallas_call(
        functools.partial(last_sums_kernel, slots),
        grid=(SOURCES // step_sources,),
        in_specs=[
            *half_specs(step_sources, 1)[:4],
            pl.BlockSpec((8, 16, CODES), lambda i: (0, 0, 0)),
            pl.BlockSpec((8, CODES), lambda i: (0, 0)),
        ],
        out_specs=pl.BlockSpec((OWNERS, 24, 128), lambda i: (0, 0, 0)),
        out_shape=jax.ShapeDtypeStruct((OWNERS, 24, 128), F32),
        scratch_shapes=[pltpu.VMEM((2, 272, 256), F32)],
        compiler_params=params(60),
        cost_estimate=cost(4e9, 9 * MIB),
    )(rows, picked, ids, targets, sums, counts)


def last_errors_kernel(slots, rows_ref, pick_ref, ids_ref, book_ref, before_ref, out_ref):
    del before_ref
    resid = residual(rows_ref, pick_ref, slots)
    flipped = resid.astype(F32).T
    for m, line in enumerate(least_errors(slots, resid, flipped, ids_ref[...] >= 0, book_ref)):
        out_ref[m : m + 1, :] = line


def last_errors(begin, end, rows, picked, ids, book, before):
    step_sources = 32
    slots = step_sources * CAP
    specs = half_specs(step_sources, 1, begin)
    return pl.pallas_call(
        functools.partial(last_errors_kernel, slots),
        grid=(end - begin,),
        in_specs=[*specs[:3], specs[4], pl.BlockSpec(memory_space=pl.ANY)],
        out_specs=pl.BlockSpec((8, slots), lambda i: (1, i + begin)),
        out_shape=jax.ShapeDtypeStruct((16, SLOTS), F32),
        input_output_aliases={4: 0},
        compiler_params=params(60),
        cost_estimate=cost(4.4e9 * (end - begin), (end - begin) * 3 * MIB),
    )(rows, picked, ids, book, before)


def new_piece(got, codes):
    total = jnp.sum(got, axis=0)
    low = (codes[:, :128] + total[:8]) / (1.0 + total[16:17])
    high = (codes[:, 128:] + total[8:16]) / (1.0 + total[17:18])
    piece = jnp.concatenate([low, high], axis=1)
    return jnp.broadcast_to(piece[None], (OWNERS, 8, CODES))


def exchange(x, axes):
    return lax.all_to_all(x, axes, split_axis=0, concat_axis=0, tiled=True)


def per_device(
    embeddings, owner_of_row, list_in_owner, opq_matrix, centroids, codebook, code_targets
):
    every = ("sub", "lists")
    owner = owner_of_row.reshape(1, ROWS)
    lists = list_in_owner.reshape(1, ROWS)
    send0, place, start = route(0, owner, lists, embeddings, opq_matrix)
    rows0 = exchange(send0.reshape(SOURCES, CAP + ID_ROWS, 128), every)
    (send1,) = route(1, start, place, embeddings, opq_matrix)
    book = make_book(codebook)
    me = lax.axis_index("lists")
    codes = codebook.astype(F32).reshape(OWNERS, 8, CODES)
    codes = lax.dynamic_slice(codes, (me, 0, 0), (1, 8, CODES))[0]
    send1, book, codes = lax.optimization_barrier((send1, book, codes))
    rows1 = exchange(send1.reshape(SOURCES, CAP, 128), every)
    picked, ids = pick(rows0, centroids)
    quant_error, sums, counts = first_half(rows0, picked, ids, code_targets, book)
    rows1, quant_error, sums = lax.optimization_barrier((rows1, quant_error, sums))
    pieces = last_sums(rows1, picked, ids, code_targets, sums, counts)
    quant_error = last_errors(0, 2, rows1, picked, ids, book, quant_error)
    got = exchange(pieces, "lists")
    piece, quant_error = lax.optimization_barrier((new_piece(got, codes), quant_error))
    spread = exchange(piece, "lists")
    quant_error = last_errors(2, 4, rows1, picked, ids, book, quant_error)
    return quant_error, spread.reshape(16, 16, CODES)


def solution(mesh):
    placed = (
        P(("lists", "sub"), None),
        P(("lists", "sub"), None),
        P(("lists", "sub")),
        P(),
        P("lists", "sub"),
        P("sub", None, None),
        P("sub", "lists"),
    )
    return jax.shard_map(
        per_device,
        mesh=mesh,
        in_specs=placed,
        out_specs=(P("sub", "lists"), P("sub", None, None)),
        check_vma=False,
    )
```

```python
import functools

import jax
import jax.numpy as jnp
from jax import lax
from jax.experimental import pallas as pl
from jax.experimental.pallas import tpu as pltpu
from jax.sharding import PartitionSpec as P

BF = jnp.bfloat16
F32 = jnp.float32
I32 = jnp.int32
I16 = jnp.int16
OWNERS = 32
GROUPS = 4
CAP = 128
ROWS = 2048
WIDTH = 1024
SOURCES = OWNERS * GROUPS
SLOTS = SOURCES * CAP
LISTS = 2048
CODES = 256
MIB = 2**20


def nn(a, b):
    return jnp.dot(a, b, preferred_element_type=F32)


def nt(a, b):
    return lax.dot_general(a, b, (((1,), (1,)), ((), ())), preferred_element_type=F32)


def params(mib):
    return pltpu.CompilerParams(
        vmem_limit_bytes=mib * MIB, dimension_semantics=("arbitrary",)
    )


def cost(flops, bytes_accessed):
    return pl.CostEstimate(
        flops=int(flops), bytes_accessed=int(bytes_accessed), transcendentals=0
    )


ORDERED = ROWS + 16 * OWNERS
ID_ROWS = 8


def rank_rows(owner, lists):
    owner_hot = (owner == lax.broadcasted_iota(I32, (OWNERS, ROWS), 0)).astype(F32)
    before = (
        lax.broadcasted_iota(I32, (128, 128), 0) < lax.broadcasted_iota(I32, (128, 128), 1)
    ).astype(F32)
    blocks = ROWS // 128
    stacked = jnp.concatenate(
        [owner_hot[:, b * 128 : (b + 1) * 128] for b in range(blocks)], axis=0
    ).astype(BF)
    inside = nn(stacked, before.astype(BF))
    ranks = []
    carry = jnp.zeros((OWNERS, 1), F32)
    for b in range(blocks):
        hot = owner_hot[:, b * 128 : (b + 1) * 128]
        earlier = inside[b * OWNERS : (b + 1) * OWNERS] + carry
        ranks.append(jnp.sum(hot * earlier, axis=0, keepdims=True))
        carry = carry + jnp.sum(hot, axis=1, keepdims=True)
    rank = jnp.concatenate(ranks, axis=1)
    pages = ((carry.astype(I32) + 15) // 16).astype(F32).astype(BF)
    after = before[:OWNERS, :OWNERS].T.astype(BF)
    first = nn(after, jnp.broadcast_to(pages, (OWNERS, 128)))
    begin = jnp.sum(owner_hot * first[:, :1], axis=0, keepdims=True) * 16.0
    place = (begin + rank).astype(I32)
    rank = rank.astype(I32)
    rank_hot = (rank == lax.broadcasted_iota(I32, (CAP, ROWS), 0)).astype(F32).astype(BF)
    high = (lists // 128).astype(F32)
    low = (lists % 128).astype(F32)
    left = jnp.concatenate([owner_hot * high, owner_hot * low, owner_hot], axis=0).astype(BF)
    found = nt(left, rank_hot)
    number = found[:OWNERS] * 128.0 + found[OWNERS : 2 * OWNERS]
    ids = (number + found[2 * OWNERS :] - 1.0).astype(I32)
    return place, first.astype(I32), ids


def matrix_columns(half):
    return [
        pl.BlockSpec((WIDTH, 128), functools.partial(lambda col, i: (0, col), 2 * g + half))
        for g in range(GROUPS)
    ]


def order_rows(place, rot_ref, run_ref, row_steps):
    run_rows = ORDERED // row_steps
    one = jnp.ones((), BF)
    zero = jnp.zeros((), BF)
    digit = lax.broadcasted_iota(I32, (run_rows, ROWS), 0).astype(I16)
    for k in range(row_steps):
        hot = jnp.where((place - k * run_rows).astype(I16) == digit, one, zero)
        run_ref[k * run_rows : (k + 1) * run_rows, :] = nn(hot, rot_ref[...]).astype(BF)
    run_ref[ORDERED:, :] = jnp.zeros((CAP, GROUPS * 128), BF)


def route_kernel(half, parts, row_steps, step_owners, *refs):
    if half == 0:
        owner_ref, list_ref, rows_hbm, r0, r1, r2, r3, out_ref, place_ref, first_ref = refs[:10]
        start_ref, ids_ref, rows_ref, rot_ref, run_ref, in_sem, start_sem = refs[10:]
    else:
        start_ref, place_ref, rows_hbm, r0, r1, r2, r3, out_ref = refs[:8]
        rows_ref, rot_ref, run_ref, in_sem = refs[8:]
    step = pl.program_id(0)
    part_rows = ROWS // parts

    @pl.when(step == 0)
    def _():
        copies = []
        for k in range(parts):
            part = pl.ds(k * part_rows, part_rows)
            copies.append(
                pltpu.make_async_copy(rows_hbm.at[part], rows_ref.at[part], in_sem.at[k])
            )
            copies[k].start()
        if half == 0:
            place, first, ids = rank_rows(owner_ref[...], list_ref[...])
            place_ref[...] = place
            first_ref[...] = first
            ids_ref[...] = ids
            starts = pltpu.make_async_copy(first_ref, start_ref, start_sem)
            starts.start()
        matrix = jnp.concatenate([r[...] for r in (r0, r1, r2, r3)], axis=1)
        for k in range(parts):
            part = pl.ds(k * part_rows, part_rows)
            copies[k].wait()
            rot_ref[part, :] = nn(rows_ref[part, :], matrix).astype(BF)
        order_rows(place_ref[...], rot_ref, run_ref, row_steps)
        if half == 0:
            starts.wait()

    line = lax.broadcasted_iota(I32, (ID_ROWS, CAP), 0)
    for j in range(step_owners):
        owner = step * step_owners + j
        begin = pl.multiple_of(start_ref[owner, 0] * 16, 16)
        run = run_ref[pl.ds(begin, CAP), :]
        for g in range(GROUPS):
            out_ref[g, j, :CAP, :] = run[:, g * 128 : (g + 1) * 128]
        if half == 0:
            ids = ids_ref[pl.ds(owner, 1), :]
            high = jnp.where(ids < 0, -1, ids // 128)
            low = ids % 128
            tail = jnp.where(line == 0, high, jnp.where(line == 1, low, 0))
            tail = tail.astype(F32).astype(BF)
            for g in range(GROUPS):
                out_ref[g, j, CAP:, :] = tail


def route(half, first_arg, second_arg, embeddings, matrix):
    step_owners = 8
    parts = 4
    row_steps = 5
    depth = CAP + (ID_ROWS if half == 0 else 0)
    line = pl.BlockSpec((1, ROWS), lambda i: (0, 0))
    out_specs = [pl.BlockSpec((GROUPS, step_owners, depth, 128), lambda i: (0, i, 0, 0))]
    out_shape = [jax.ShapeDtypeStruct((GROUPS, OWNERS, depth, 128), BF)]
    scratch = [
        pltpu.VMEM((ROWS, WIDTH), BF),
        pltpu.VMEM((ROWS, GROUPS * 128), BF),
        pltpu.VMEM((ORDERED + CAP, GROUPS * 128), BF),
        pltpu.SemaphoreType.DMA((parts,)),
    ]
    if half == 0:
        inputs = [line, line]
        out_specs += [line, pl.BlockSpec((OWNERS, 128), lambda i: (0, 0))]
        out_shape += [
            jax.ShapeDtypeStruct((1, ROWS), I32),
            jax.ShapeDtypeStruct((OWNERS, 128), I32),
        ]
        scratch = [
            pltpu.SMEM((OWNERS, 128), I32),
            pltpu.VMEM((OWNERS, CAP), I32),
            *scratch,
            pltpu.SemaphoreType.DMA,
        ]
    else:
        inputs = [pl.BlockSpec(memory_space=pltpu.SMEM), line]
    return pl.pallas_call(
        functools.partial(route_kernel, half, parts, row_steps, step_owners),
        grid=(OWNERS // step_owners,),
        in_specs=[*inputs, pl.BlockSpec(memory_space=pl.ANY), *matrix_columns(half)],
        out_specs=out_specs,
        out_shape=out_shape,
        scratch_shapes=scratch,
        compiler_params=params(60),
        cost_estimate=cost(8e9, 10 * MIB),
    )(first_arg, second_arg, embeddings, matrix, matrix, matrix, matrix)


def pick_kernel(step_sources, tail_ref, centroid_ref, out_ref, ids_ref):
    one = jnp.ones((), BF)
    zero = jnp.zeros((), BF)
    lane = lax.broadcasted_iota(I32, (CAP, 128), 1).astype(I16)
    numbers = []
    hots = []
    for j in range(step_sources):
        tail = tail_ref[j, CAP:, :].astype(F32)
        number = tail[0:1, :] * 128.0 + tail[1:2, :]
        numbers.append(number)
        column = jnp.broadcast_to(number, (128, CAP)).T.astype(I32).astype(I16)
        hots.append(
            jnp.concatenate(
                [
                    jnp.where(column == lane + jnp.int16(128 * b), one, zero)
                    for b in range(LISTS // 128)
                ],
                axis=1,
            )
        )
    found = nn(jnp.concatenate(hots, axis=0), centroid_ref[...]).astype(BF)
    out_ref[...] = found.reshape(step_sources, CAP, 256)
    ids_ref[...] = jnp.concatenate(numbers, axis=1)


def pick(rows0, centroids):
    step_sources = 16
    slots = step_sources * CAP
    return pl.pallas_call(
        functools.partial(pick_kernel, step_sources),
        grid=(SOURCES // step_sources,),
        in_specs=[
            pl.BlockSpec((step_sources, CAP + ID_ROWS, CAP), lambda i: (i, 0, 0)),
            pl.BlockSpec((LISTS, 256), lambda i: (0, 0)),
        ],
        out_specs=[
            pl.BlockSpec((step_sources, CAP, 256), lambda i: (i, 0, 0)),
            pl.BlockSpec((1, slots), lambda i: (0, i)),
        ],
        out_shape=[
            jax.ShapeDtypeStruct((SOURCES, CAP, 256), BF),
            jax.ShapeDtypeStruct((1, SLOTS), F32),
        ],
        compiler_params=params(60),
        cost_estimate=cost(18e9, 14 * MIB),
    )(rows0, centroids)


def book_kernel(code_ref, out_ref):
    codes = code_ref[...].astype(F32).T
    lane = lax.broadcasted_iota(I32, (CODES, 128), 1)
    for m in range(8):
        mine = jnp.where(lane // 16 == m, codes, 0.0)
        square = jnp.sum(mine * mine, axis=1, keepdims=True)
        high = square.astype(BF).astype(F32)
        middle = (square - high).astype(BF).astype(F32)
        low = square - high - middle
        tail = jnp.where(
            lane == 0, high, jnp.where(lane == 1, middle, jnp.where(lane == 2, low, 0.0))
        )
        out_ref[m * CODES : (m + 1) * CODES, :128] = (-2.0 * mine).astype(BF)
        out_ref[m * CODES : (m + 1) * CODES, 128:] = tail.astype(BF)


def make_book(codebook):
    return pl.pallas_call(
        book_kernel,
        grid=(2,),
        in_specs=[pl.BlockSpec((128, CODES), lambda i: (i, 0))],
        out_specs=pl.BlockSpec((8 * CODES, 256), lambda i: (i, 0)),
        out_shape=jax.ShapeDtypeStruct((16 * CODES, 256), BF),
        compiler_params=params(60),
        cost_estimate=cost(1e9, 3 * MIB),
    )(codebook.reshape(256, CODES))


def residual(rows_ref, pick_ref, slots):
    rows = rows_ref[...].reshape(slots, 128).astype(F32)
    centre = pick_ref[...].reshape(slots, 128).astype(F32)
    return (rows - centre).astype(BF)


def add_sums(slots, flipped, live, target, acc_ref):
    high = jnp.where(live, target // 64, -1).astype(I16)
    low = (target % 64).astype(I16)
    digit = lax.broadcasted_iota(I32, (64, slots), 0).astype(I16)
    line = lax.broadcasted_iota(I32, (16, slots), 0)
    nth = (line // 4).astype(I16)
    quarter = (line % 4).astype(I16)
    one = jnp.ones((), BF)
    zero = jnp.zeros((), BF)
    for t in range(2):
        left = []
        right = []
        mixed = jnp.zeros((16, slots), I16)
        for m in range(4 * t, 4 * t + 4):
            mine = flipped[m * 16 : (m + 1) * 16]
            row = jnp.broadcast_to(high[m : m + 1], (16, slots))
            mixed = jnp.where(nth == jnp.int16(m % 4), row, mixed)
            for h in range(4):
                left.append(jnp.where(row == jnp.int16(h), mine, zero))
            right.append(jnp.where(low[m : m + 1] == digit, one, zero))
        left.append(jnp.where(mixed == quarter, one, zero))
        acc_ref[t] += nt(jnp.concatenate(left, axis=0), jnp.concatenate(right, axis=0))


def sum_of(acc_ref, m):
    base = (m % 4) * 64
    part = acc_ref[m // 4][:, base : base + 64]
    return jnp.concatenate([part[base + h * 16 : base + (h + 1) * 16] for h in range(4)], axis=1)


def count_of(acc_ref, m):
    base = (m % 4) * 64
    part = acc_ref[m // 4][256:, base : base + 64]
    at = (m % 4) * 4
    return jnp.concatenate([part[at + h : at + h + 1] for h in range(4)], axis=1)


def least_errors(slots, resid, flipped, live, book_ref):
    wide = jnp.concatenate([resid, jnp.ones((slots, 128), BF)], axis=1)
    lines = []
    for m in range(8):
        mine = flipped[m * 16 : (m + 1) * 16].astype(F32)
        row_sq = jnp.sum(mine * mine, axis=0, keepdims=True)
        dist = nt(book_ref[m * CODES : (m + 1) * CODES], wide)
        least = jnp.min(dist, axis=0, keepdims=True)
        lines.append(jnp.where(live, row_sq + least, 0.0))
    return lines


def half_specs(step_sources, half, begin=0):
    slots = step_sources * CAP
    return [
        pl.BlockSpec((step_sources, CAP, 128), lambda i: (i + begin, 0, 0)),
        pl.BlockSpec((step_sources, CAP, 128), lambda i: (i + begin, 0, half)),
        pl.BlockSpec((1, slots), lambda i: (0, i + begin)),
        pl.BlockSpec((8, slots), lambda i: (half, i + begin)),
        pl.BlockSpec((8 * CODES, 256), lambda i: (half, 0)),
    ]


def first_half_kernel(slots, rows_ref, pick_ref, ids_ref, target_ref, book_ref,
                      error_ref, sum_ref, count_ref, acc_ref):
    step = pl.program_id(0)

    @pl.when(step == 0)
    def _():
        acc_ref[...] = jnp.zeros_like(acc_ref)

    resid = residual(rows_ref, pick_ref, slots)
    flipped = resid.T
    live = ids_ref[...] >= 0
    add_sums(slots, flipped, live, target_ref[...], acc_ref)
    for m, line in enumerate(least_errors(slots, resid, flipped, live, book_ref)):
        error_ref[m : m + 1, :] = line

    @pl.when(step == pl.num_programs(0) - 1)
    def _():
        for m in range(8):
            sum_ref[m] = sum_of(acc_ref, m)
            count_ref[m : m + 1, :] = count_of(acc_ref, m)


def first_half(rows, picked, ids, targets, book):
    step_sources = 32
    slots = step_sources * CAP
    return pl.pallas_call(
        functools.partial(first_half_kernel, slots),
        grid=(SOURCES // step_sources,),
        in_specs=half_specs(step_sources, 0),
        out_specs=[
            pl.BlockSpec((8, slots), lambda i: (0, i)),
            pl.BlockSpec((8, 16, CODES), lambda i: (0, 0, 0)),
            pl.BlockSpec((8, CODES), lambda i: (0, 0)),
        ],
        out_shape=[
            jax.ShapeDtypeStruct((16, SLOTS), F32),
            jax.ShapeDtypeStruct((8, 16, CODES), F32),
            jax.ShapeDtypeStruct((8, CODES), F32),
        ],
        scratch_shapes=[pltpu.VMEM((2, 272, 256), F32)],
        compiler_params=params(60),
        cost_estimate=cost(22e9, 10 * MIB),
    )(rows, picked, ids, targets, book)


def last_sums_kernel(slots, rows_ref, pick_ref, ids_ref, target_ref, sum_ref, count_ref, out_ref, acc_ref):
    step = pl.program_id(0)

    @pl.when(step == 0)
    def _():
        acc_ref[...] = jnp.zeros_like(acc_ref)
        out_ref[:, 16:, :] = jnp.zeros((OWNERS, 8, 128), F32)

    resid = residual(rows_ref, pick_ref, slots)
    flipped = resid.T
    add_sums(slots, flipped, ids_ref[...] >= 0, target_ref[...], acc_ref)

    @pl.when(step == pl.num_programs(0) - 1)
    def _():
        for m in range(16):
            total = sum_ref[m] if m < 8 else sum_of(acc_ref, m - 8)
            count = count_ref[m : m + 1, :] if m < 8 else count_of(acc_ref, m - 8)
            for h in range(2):
                out_ref[2 * m + h, :8, :] = total[8 * h : 8 * h + 8, :128]
                out_ref[2 * m + h, 8:16, :] = total[8 * h : 8 * h + 8, 128:]
                out_ref[2 * m + h, 16:17, :] = count[:, :128]
                out_ref[2 * m + h, 17:18, :] = count[:, 128:]


def last_sums(rows, picked, ids, targets, sums, counts):
    step_sources = 32
    slots = step_sources * CAP
    return pl.pallas_call(
        functools.partial(last_sums_kernel, slots),
        grid=(SOURCES // step_sources,),
        in_specs=[
            *half_specs(step_sources, 1)[:4],
            pl.BlockSpec((8, 16, CODES), lambda i: (0, 0, 0)),
            pl.BlockSpec((8, CODES), lambda i: (0, 0)),
        ],
        out_specs=pl.BlockSpec((OWNERS, 24, 128), lambda i: (0, 0, 0)),
        out_shape=jax.ShapeDtypeStruct((OWNERS, 24, 128), F32),
        scratch_shapes=[pltpu.VMEM((2, 272, 256), F32)],
        compiler_params=params(60),
        cost_estimate=cost(4e9, 9 * MIB),
    )(rows, picked, ids, targets, sums, counts)


def last_errors_kernel(slots, rows_ref, pick_ref, ids_ref, book_ref, before_ref, out_ref):
    del before_ref
    blocks = 4
    part = slots // blocks
    for b in range(blocks):
        sources = slice(b * part // CAP, (b + 1) * part // CAP)
        at = slice(b * part, (b + 1) * part)
        resid = residual(rows_ref.at[sources], pick_ref.at[sources], part)
        live = ids_ref[:, at] >= 0
        for m, line in enumerate(least_errors(part, resid, resid.T, live, book_ref)):
            out_ref[m : m + 1, at] = line


def last_errors(begin, end, rows, picked, ids, book, before):
    step_sources = 32
    slots = step_sources * CAP
    specs = half_specs(step_sources, 1, begin)
    return pl.pallas_call(
        functools.partial(last_errors_kernel, slots),
        grid=(end - begin,),
        in_specs=[*specs[:3], specs[4], pl.BlockSpec(memory_space=pl.ANY)],
        out_specs=pl.BlockSpec((8, slots), lambda i: (1, i + begin)),
        out_shape=jax.ShapeDtypeStruct((16, SLOTS), F32),
        input_output_aliases={4: 0},
        compiler_params=params(60),
        cost_estimate=cost(4.4e9 * (end - begin), (end - begin) * 3 * MIB),
    )(rows, picked, ids, book, before)


def new_piece(got, codes):
    total = jnp.sum(got, axis=0)
    low = (codes[:, :128] + total[:8]) / (1.0 + total[16:17])
    high = (codes[:, 128:] + total[8:16]) / (1.0 + total[17:18])
    piece = jnp.concatenate([low, high], axis=1)
    return jnp.broadcast_to(piece[None], (OWNERS, 8, CODES))


def exchange(x, axes):
    return lax.all_to_all(x, axes, split_axis=0, concat_axis=0, tiled=True)


def per_device(
    embeddings, owner_of_row, list_in_owner, opq_matrix, centroids, codebook, code_targets
):
    every = ("sub", "lists")
    owner = owner_of_row.reshape(1, ROWS)
    lists = list_in_owner.reshape(1, ROWS)
    send0, place, start = route(0, owner, lists, embeddings, opq_matrix)
    rows0 = exchange(send0.reshape(SOURCES, CAP + ID_ROWS, 128), every)
    (send1,) = route(1, start, place, embeddings, opq_matrix)
    book = make_book(codebook)
    me = lax.axis_index("lists")
    codes = codebook.astype(F32).reshape(OWNERS, 8, CODES)
    codes = lax.dynamic_slice(codes, (me, 0, 0), (1, 8, CODES))[0]
    send1, book, codes = lax.optimization_barrier((send1, book, codes))
    rows1 = exchange(send1.reshape(SOURCES, CAP, 128), every)
    picked, ids = pick(rows0, centroids)
    quant_error, sums, counts = first_half(rows0, picked, ids, code_targets, book)
    rows1, quant_error, sums = lax.optimization_barrier((rows1, quant_error, sums))
    pieces = last_sums(rows1, picked, ids, code_targets, sums, counts)
    quant_error = last_errors(0, 2, rows1, picked, ids, book, quant_error)
    got = exchange(pieces, "lists")
    piece, quant_error = lax.optimization_barrier((new_piece(got, codes), quant_error))
    spread = exchange(piece, "lists")
    quant_error = last_errors(2, 4, rows1, picked, ids, book, quant_error)
    return quant_error, spread.reshape(16, 16, CODES)


def solution(mesh):
    placed = (
        P(("lists", "sub"), None),
        P(("lists", "sub"), None),
        P(("lists", "sub")),
        P(),
        P("lists", "sub"),
        P("sub", None, None),
        P("sub", "lists"),
    )
    return jax.shard_map(
        per_device,
        mesh=mesh,
        in_specs=placed,
        out_specs=(P("sub", "lists"), P("sub", None, None)),
        check_vma=False,
    )
```

```python
import functools

import jax
import jax.numpy as jnp
from jax import lax
from jax.experimental import pallas as pl
from jax.experimental.pallas import tpu as pltpu
from jax.sharding import PartitionSpec as P

BF = jnp.bfloat16
F32 = jnp.float32
I32 = jnp.int32
I16 = jnp.int16
OWNERS = 32
GROUPS = 4
CAP = 128
ROWS = 2048
WIDTH = 1024
SOURCES = OWNERS * GROUPS
SLOTS = SOURCES * CAP
LISTS = 2048
CODES = 256
MIB = 2**20


def nn(a, b):
    return jnp.dot(a, b, preferred_element_type=F32)


def nt(a, b):
    return lax.dot_general(a, b, (((1,), (1,)), ((), ())), preferred_element_type=F32)


def params(mib):
    return pltpu.CompilerParams(
        vmem_limit_bytes=mib * MIB, dimension_semantics=("arbitrary",)
    )


def cost(flops, bytes_accessed):
    return pl.CostEstimate(
        flops=int(flops), bytes_accessed=int(bytes_accessed), transcendentals=0
    )


ORDERED = ROWS + 16 * OWNERS
ID_ROWS = 16


def rank_rows(owner, lists):
    owner_hot = (owner == lax.broadcasted_iota(I32, (OWNERS, ROWS), 0)).astype(F32)
    before = (
        lax.broadcasted_iota(I32, (128, 128), 0) < lax.broadcasted_iota(I32, (128, 128), 1)
    ).astype(F32)
    blocks = ROWS // 128
    stacked = jnp.concatenate(
        [owner_hot[:, b * 128 : (b + 1) * 128] for b in range(blocks)], axis=0
    ).astype(BF)
    inside = nn(stacked, before.astype(BF))
    ranks = []
    carry = jnp.zeros((OWNERS, 1), F32)
    for b in range(blocks):
        hot = owner_hot[:, b * 128 : (b + 1) * 128]
        earlier = inside[b * OWNERS : (b + 1) * OWNERS] + carry
        ranks.append(jnp.sum(hot * earlier, axis=0, keepdims=True))
        carry = carry + jnp.sum(hot, axis=1, keepdims=True)
    rank = jnp.concatenate(ranks, axis=1)
    pages = ((carry.astype(I32) + 15) // 16).astype(F32).astype(BF)
    after = before[:OWNERS, :OWNERS].T.astype(BF)
    first = nn(after, jnp.broadcast_to(pages, (OWNERS, 128)))
    begin = jnp.sum(owner_hot * first[:, :1], axis=0, keepdims=True) * 16.0
    place = (begin + rank).astype(I32)
    rank = rank.astype(I32)
    rank_hot = (rank == lax.broadcasted_iota(I32, (CAP, ROWS), 0)).astype(F32).astype(BF)
    high = (lists // 128).astype(F32)
    low = (lists % 128).astype(F32)
    left = jnp.concatenate([owner_hot * high, owner_hot * low, owner_hot], axis=0).astype(BF)
    found = nt(left, rank_hot)
    number = found[:OWNERS] * 128.0 + found[OWNERS : 2 * OWNERS]
    ids = (number + found[2 * OWNERS :] - 1.0).astype(I32)
    return place, first.astype(I32), ids


def matrix_columns(half):
    return [
        pl.BlockSpec((WIDTH, 128), functools.partial(lambda col, i: (0, col), 2 * g + half))
        for g in range(GROUPS)
    ]


def order_rows(place, rot_ref, run_ref, row_steps):
    run_rows = ORDERED // row_steps
    one = jnp.ones((), BF)
    zero = jnp.zeros((), BF)
    digit = lax.broadcasted_iota(I32, (run_rows, ROWS), 0).astype(I16)
    for k in range(row_steps):
        hot = jnp.where((place - k * run_rows).astype(I16) == digit, one, zero)
        run_ref[k * run_rows : (k + 1) * run_rows, :] = nn(hot, rot_ref[...]).astype(BF)
    run_ref[ORDERED:, :] = jnp.zeros((CAP, GROUPS * 128), BF)


def route_kernel(half, parts, row_steps, step_owners, *refs):
    if half == 0:
        owner_ref, list_ref, rows_hbm, r0, r1, r2, r3, out_ref, place_ref, first_ref = refs[:10]
        start_ref, ids_ref, rows_ref, rot_ref, run_ref, in_sem, start_sem = refs[10:]
    else:
        start_ref, place_ref, rows_hbm, r0, r1, r2, r3, out_ref = refs[:8]
        rows_ref, rot_ref, run_ref, in_sem = refs[8:]
    step = pl.program_id(0)
    part_rows = ROWS // parts

    @pl.when(step == 0)
    def _():
        copies = []
        for k in range(parts):
            part = pl.ds(k * part_rows, part_rows)
            copies.append(
                pltpu.make_async_copy(rows_hbm.at[part], rows_ref.at[part], in_sem.at[k])
            )
            copies[k].start()
        if half == 0:
            place, first, ids = rank_rows(owner_ref[...], list_ref[...])
            place_ref[...] = place
            first_ref[...] = first
            ids_ref[...] = ids
            starts = pltpu.make_async_copy(first_ref, start_ref, start_sem)
            starts.start()
        matrix = jnp.concatenate([r[...] for r in (r0, r1, r2, r3)], axis=1)
        for k in range(parts):
            part = pl.ds(k * part_rows, part_rows)
            copies[k].wait()
            rot_ref[part, :] = nn(rows_ref[part, :], matrix).astype(BF)
        order_rows(place_ref[...], rot_ref, run_ref, row_steps)
        if half == 0:
            starts.wait()

    line = lax.broadcasted_iota(I32, (ID_ROWS, CAP), 0)
    for j in range(step_owners):
        owner = step * step_owners + j
        begin = pl.multiple_of(start_ref[owner, 0] * 16, 16)
        run = run_ref[pl.ds(begin, CAP), :]
        for g in range(GROUPS):
            out_ref[g, j, :CAP, :] = run[:, g * 128 : (g + 1) * 128]
        if half == 0:
            ids = ids_ref[pl.ds(owner, 1), :]
            high = jnp.where(ids < 0, -1, ids // 128)
            low = ids % 128
            tail = jnp.where(line == 0, high, jnp.where(line == 1, low, 0))
            tail = tail.astype(F32).astype(BF)
            for g in range(GROUPS):
                out_ref[g, j, CAP:, :] = tail


def route(half, first_arg, second_arg, embeddings, matrix):
    step_owners = 16
    parts = 4
    row_steps = 5
    depth = CAP + (ID_ROWS if half == 0 else 0)
    line = pl.BlockSpec((1, ROWS), lambda i: (0, 0))
    out_specs = [pl.BlockSpec((GROUPS, step_owners, depth, 128), lambda i: (0, i, 0, 0))]
    out_shape = [jax.ShapeDtypeStruct((GROUPS, OWNERS, depth, 128), BF)]
    scratch = [
        pltpu.VMEM((ROWS, WIDTH), BF),
        pltpu.VMEM((ROWS, GROUPS * 128), BF),
        pltpu.VMEM((ORDERED + CAP, GROUPS * 128), BF),
        pltpu.SemaphoreType.DMA((parts,)),
    ]
    if half == 0:
        inputs = [line, line]
        out_specs += [line, pl.BlockSpec((OWNERS, 128), lambda i: (0, 0))]
        out_shape += [
            jax.ShapeDtypeStruct((1, ROWS), I32),
            jax.ShapeDtypeStruct((OWNERS, 128), I32),
        ]
        scratch = [
            pltpu.SMEM((OWNERS, 128), I32),
            pltpu.VMEM((OWNERS, CAP), I32),
            *scratch,
            pltpu.SemaphoreType.DMA,
        ]
    else:
        inputs = [pl.BlockSpec(memory_space=pltpu.SMEM), line]
    return pl.pallas_call(
        functools.partial(route_kernel, half, parts, row_steps, step_owners),
        grid=(OWNERS // step_owners,),
        in_specs=[*inputs, pl.BlockSpec(memory_space=pl.ANY), *matrix_columns(half)],
        out_specs=out_specs,
        out_shape=out_shape,
        scratch_shapes=scratch,
        compiler_params=params(60),
        cost_estimate=cost(8e9, 10 * MIB),
    )(first_arg, second_arg, embeddings, matrix, matrix, matrix, matrix)


def pick_kernel(step_sources, tail_ref, centroid_ref, out_ref, ids_ref):
    one = jnp.ones((), BF)
    zero = jnp.zeros((), BF)
    lane = lax.broadcasted_iota(I32, (CAP, 128), 1).astype(I16)
    numbers = []
    hots = []
    for j in range(step_sources):
        tail = tail_ref[j, CAP:, :].astype(F32)
        number = tail[0:1, :] * 128.0 + tail[1:2, :]
        numbers.append(number)
        column = jnp.broadcast_to(number, (128, CAP)).T.astype(I32).astype(I16)
        hots.append(
            jnp.concatenate(
                [
                    jnp.where(column == lane + jnp.int16(128 * b), one, zero)
                    for b in range(LISTS // 128)
                ],
                axis=1,
            )
        )
    found = nn(jnp.concatenate(hots, axis=0), centroid_ref[...]).astype(BF)
    out_ref[...] = found.reshape(step_sources, CAP, 256)
    ids_ref[...] = jnp.concatenate(numbers, axis=1)


def pick(rows0, centroids):
    step_sources = 16
    slots = step_sources * CAP
    return pl.pallas_call(
        functools.partial(pick_kernel, step_sources),
        grid=(SOURCES // step_sources,),
        in_specs=[
            pl.BlockSpec((step_sources, CAP + ID_ROWS, CAP), lambda i: (i, 0, 0)),
            pl.BlockSpec((LISTS, 256), lambda i: (0, 0)),
        ],
        out_specs=[
            pl.BlockSpec((step_sources, CAP, 256), lambda i: (i, 0, 0)),
            pl.BlockSpec((1, slots), lambda i: (0, i)),
        ],
        out_shape=[
            jax.ShapeDtypeStruct((SOURCES, CAP, 256), BF),
            jax.ShapeDtypeStruct((1, SLOTS), F32),
        ],
        compiler_params=params(60),
        cost_estimate=cost(18e9, 14 * MIB),
    )(rows0, centroids)


def book_kernel(code_ref, out_ref):
    codes = code_ref[...].astype(F32).T
    lane = lax.broadcasted_iota(I32, (CODES, 128), 1)
    for m in range(8):
        mine = jnp.where(lane // 16 == m, codes, 0.0)
        square = jnp.sum(mine * mine, axis=1, keepdims=True)
        high = square.astype(BF).astype(F32)
        middle = (square - high).astype(BF).astype(F32)
        low = square - high - middle
        tail = jnp.where(
            lane == 0, high, jnp.where(lane == 1, middle, jnp.where(lane == 2, low, 0.0))
        )
        out_ref[m * CODES : (m + 1) * CODES, :128] = (-2.0 * mine).astype(BF)
        out_ref[m * CODES : (m + 1) * CODES, 128:] = tail.astype(BF)


def make_book(codebook):
    return pl.pallas_call(
        book_kernel,
        grid=(2,),
        in_specs=[pl.BlockSpec((128, CODES), lambda i: (i, 0))],
        out_specs=pl.BlockSpec((8 * CODES, 256), lambda i: (i, 0)),
        out_shape=jax.ShapeDtypeStruct((16 * CODES, 256), BF),
        compiler_params=params(60),
        cost_estimate=cost(1e9, 3 * MIB),
    )(codebook.reshape(256, CODES))


def residual(rows_ref, pick_ref, slots):
    rows = rows_ref[...].reshape(slots, 128).astype(F32)
    centre = pick_ref[...].reshape(slots, 128).astype(F32)
    return (rows - centre).astype(BF)


def add_sums(slots, flipped, live, target, acc_ref):
    high = jnp.where(live, target // 64, -1).astype(I16)
    low = (target % 64).astype(I16)
    digit = lax.broadcasted_iota(I32, (64, slots), 0).astype(I16)
    line = lax.broadcasted_iota(I32, (16, slots), 0)
    nth = (line // 4).astype(I16)
    quarter = (line % 4).astype(I16)
    one = jnp.ones((), BF)
    zero = jnp.zeros((), BF)
    for t in range(2):
        left = []
        right = []
        mixed = jnp.zeros((16, slots), I16)
        for m in range(4 * t, 4 * t + 4):
            mine = flipped[m * 16 : (m + 1) * 16]
            row = jnp.broadcast_to(high[m : m + 1], (16, slots))
            mixed = jnp.where(nth == jnp.int16(m % 4), row, mixed)
            for h in range(4):
                left.append(jnp.where(row == jnp.int16(h), mine, zero))
            right.append(jnp.where(low[m : m + 1] == digit, one, zero))
        left.append(jnp.where(mixed == quarter, one, zero))
        acc_ref[t] += nt(jnp.concatenate(left, axis=0), jnp.concatenate(right, axis=0))


def sum_of(acc_ref, m):
    base = (m % 4) * 64
    part = acc_ref[m // 4][:, base : base + 64]
    return jnp.concatenate([part[base + h * 16 : base + (h + 1) * 16] for h in range(4)], axis=1)


def count_of(acc_ref, m):
    base = (m % 4) * 64
    part = acc_ref[m // 4][256:, base : base + 64]
    at = (m % 4) * 4
    return jnp.concatenate([part[at + h : at + h + 1] for h in range(4)], axis=1)


def least_errors(slots, resid, flipped, live, book_ref):
    wide = jnp.concatenate([resid, jnp.ones((slots, 128), BF)], axis=1)
    lines = []
    for m in range(8):
        mine = flipped[m * 16 : (m + 1) * 16].astype(F32)
        row_sq = jnp.sum(mine * mine, axis=0, keepdims=True)
        dist = nt(book_ref[m * CODES : (m + 1) * CODES], wide)
        least = jnp.min(dist, axis=0, keepdims=True)
        lines.append(jnp.where(live, row_sq + least, 0.0))
    return lines


def half_specs(step_sources, half, begin=0):
    slots = step_sources * CAP
    return [
        pl.BlockSpec((step_sources, CAP, 128), lambda i: (i + begin, 0, 0)),
        pl.BlockSpec((step_sources, CAP, 128), lambda i: (i + begin, 0, half)),
        pl.BlockSpec((1, slots), lambda i: (0, i + begin)),
        pl.BlockSpec((8, slots), lambda i: (half, i + begin)),
        pl.BlockSpec((8 * CODES, 256), lambda i: (half, 0)),
    ]


def first_half_kernel(slots, rows_ref, pick_ref, ids_ref, target_ref, book_ref,
                      error_ref, sum_ref, count_ref, acc_ref):
    step = pl.program_id(0)

    @pl.when(step == 0)
    def _():
        acc_ref[...] = jnp.zeros_like(acc_ref)

    resid = residual(rows_ref, pick_ref, slots)
    flipped = resid.T
    live = ids_ref[...] >= 0
    add_sums(slots, flipped, live, target_ref[...], acc_ref)
    for m, line in enumerate(least_errors(slots, resid, flipped, live, book_ref)):
        error_ref[m : m + 1, :] = line

    @pl.when(step == pl.num_programs(0) - 1)
    def _():
        for m in range(8):
            sum_ref[m] = sum_of(acc_ref, m)
            count_ref[m : m + 1, :] = count_of(acc_ref, m)


def first_half(rows, picked, ids, targets, book):
    step_sources = 32
    slots = step_sources * CAP
    return pl.pallas_call(
        functools.partial(first_half_kernel, slots),
        grid=(SOURCES // step_sources,),
        in_specs=half_specs(step_sources, 0),
        out_specs=[
            pl.BlockSpec((8, slots), lambda i: (0, i)),
            pl.BlockSpec((8, 16, CODES), lambda i: (0, 0, 0)),
            pl.BlockSpec((8, CODES), lambda i: (0, 0)),
        ],
        out_shape=[
            jax.ShapeDtypeStruct((16, SLOTS), F32),
            jax.ShapeDtypeStruct((8, 16, CODES), F32),
            jax.ShapeDtypeStruct((8, CODES), F32),
        ],
        scratch_shapes=[pltpu.VMEM((2, 272, 256), F32)],
        compiler_params=params(60),
        cost_estimate=cost(22e9, 10 * MIB),
    )(rows, picked, ids, targets, book)


def last_sums_kernel(slots, rows_ref, pick_ref, ids_ref, target_ref, sum_ref, count_ref, out_ref, acc_ref):
    step = pl.program_id(0)

    @pl.when(step == 0)
    def _():
        acc_ref[...] = jnp.zeros_like(acc_ref)
        out_ref[:, 16:, :] = jnp.zeros((OWNERS, 8, 128), F32)

    resid = residual(rows_ref, pick_ref, slots)
    flipped = resid.T
    add_sums(slots, flipped, ids_ref[...] >= 0, target_ref[...], acc_ref)

    @pl.when(step == pl.num_programs(0) - 1)
    def _():
        for m in range(16):
            total = sum_ref[m] if m < 8 else sum_of(acc_ref, m - 8)
            count = count_ref[m : m + 1, :] if m < 8 else count_of(acc_ref, m - 8)
            for h in range(2):
                out_ref[2 * m + h, :8, :] = total[8 * h : 8 * h + 8, :128]
                out_ref[2 * m + h, 8:16, :] = total[8 * h : 8 * h + 8, 128:]
                out_ref[2 * m + h, 16:17, :] = count[:, :128]
                out_ref[2 * m + h, 17:18, :] = count[:, 128:]


def last_sums(rows, picked, ids, targets, sums, counts):
    step_sources = 32
    slots = step_sources * CAP
    return pl.pallas_call(
        functools.partial(last_sums_kernel, slots),
        grid=(SOURCES // step_sources,),
        in_specs=[
            *half_specs(step_sources, 1)[:4],
            pl.BlockSpec((8, 16, CODES), lambda i: (0, 0, 0)),
            pl.BlockSpec((8, CODES), lambda i: (0, 0)),
        ],
        out_specs=pl.BlockSpec((OWNERS, 24, 128), lambda i: (0, 0, 0)),
        out_shape=jax.ShapeDtypeStruct((OWNERS, 24, 128), F32),
        scratch_shapes=[pltpu.VMEM((2, 272, 256), F32)],
        compiler_params=params(60),
        cost_estimate=cost(4e9, 9 * MIB),
    )(rows, picked, ids, targets, sums, counts)


def last_errors_kernel(slots, rows_ref, pick_ref, ids_ref, book_ref, before_ref, out_ref):
    del before_ref
    blocks = 4
    part = slots // blocks
    for b in range(blocks):
        sources = slice(b * part // CAP, (b + 1) * part // CAP)
        at = slice(b * part, (b + 1) * part)
        resid = residual(rows_ref.at[sources], pick_ref.at[sources], part)
        live = ids_ref[:, at] >= 0
        for m, line in enumerate(least_errors(part, resid, resid.T, live, book_ref)):
            out_ref[m : m + 1, at] = line


def last_errors(begin, end, rows, picked, ids, book, before):
    step_sources = 32
    slots = step_sources * CAP
    specs = half_specs(step_sources, 1, begin)
    return pl.pallas_call(
        functools.partial(last_errors_kernel, slots),
        grid=(end - begin,),
        in_specs=[*specs[:3], specs[4], pl.BlockSpec(memory_space=pl.ANY)],
        out_specs=pl.BlockSpec((8, slots), lambda i: (1, i + begin)),
        out_shape=jax.ShapeDtypeStruct((16, SLOTS), F32),
        input_output_aliases={4: 0},
        compiler_params=params(60),
        cost_estimate=cost(4.4e9 * (end - begin), (end - begin) * 3 * MIB),
    )(rows, picked, ids, book, before)


def new_piece(got, codes):
    total = jnp.sum(got, axis=0)
    low = (codes[:, :128] + total[:8]) / (1.0 + total[16:17])
    high = (codes[:, 128:] + total[8:16]) / (1.0 + total[17:18])
    piece = jnp.concatenate([low, high], axis=1)
    return jnp.broadcast_to(piece[None], (OWNERS, 8, CODES))


def exchange(x, axes):
    return lax.all_to_all(x, axes, split_axis=0, concat_axis=0, tiled=True)


def per_device(
    embeddings, owner_of_row, list_in_owner, opq_matrix, centroids, codebook, code_targets
):
    every = ("sub", "lists")
    owner = owner_of_row.reshape(1, ROWS)
    lists = list_in_owner.reshape(1, ROWS)
    send0, place, start = route(0, owner, lists, embeddings, opq_matrix)
    rows0 = exchange(send0.reshape(SOURCES, CAP + ID_ROWS, 128), every)
    (send1,) = route(1, start, place, embeddings, opq_matrix)
    book = make_book(codebook)
    me = lax.axis_index("lists")
    codes = codebook.astype(F32).reshape(OWNERS, 8, CODES)
    codes = lax.dynamic_slice(codes, (me, 0, 0), (1, 8, CODES))[0]
    send1, book, codes = lax.optimization_barrier((send1, book, codes))
    rows1 = exchange(send1.reshape(SOURCES, CAP, 128), every)
    picked, ids = pick(rows0, centroids)
    quant_error, sums, counts = first_half(rows0, picked, ids, code_targets, book)
    rows1, quant_error, sums = lax.optimization_barrier((rows1, quant_error, sums))
    pieces = last_sums(rows1, picked, ids, code_targets, sums, counts)
    quant_error = last_errors(0, 2, rows1, picked, ids, book, quant_error)
    got = exchange(pieces, "lists")
    piece, quant_error = lax.optimization_barrier((new_piece(got, codes), quant_error))
    spread = exchange(piece, "lists")
    quant_error = last_errors(2, 4, rows1, picked, ids, book, quant_error)
    return quant_error, spread.reshape(16, 16, CODES)


def solution(mesh):
    placed = (
        P(("lists", "sub"), None),
        P(("lists", "sub"), None),
        P(("lists", "sub")),
        P(),
        P("lists", "sub"),
        P("sub", None, None),
        P("sub", "lists"),
    )
    return jax.shard_map(
        per_device,
        mesh=mesh,
        in_specs=placed,
        out_specs=(P("sub", "lists"), P("sub", None, None)),
        check_vma=False,
    )
```

```python
import functools

import jax
import jax.numpy as jnp
from jax import lax
from jax.experimental import pallas as pl
from jax.experimental.pallas import tpu as pltpu
from jax.sharding import PartitionSpec as P

BF = jnp.bfloat16
F32 = jnp.float32
I32 = jnp.int32
I16 = jnp.int16
OWNERS = 32
GROUPS = 4
CAP = 128
ROWS = 2048
WIDTH = 1024
SOURCES = OWNERS * GROUPS
SLOTS = SOURCES * CAP
LISTS = 2048
CODES = 256
MIB = 2**20


def nn(a, b):
    return jnp.dot(a, b, preferred_element_type=F32)


def nt(a, b):
    return lax.dot_general(a, b, (((1,), (1,)), ((), ())), preferred_element_type=F32)


def params(mib):
    return pltpu.CompilerParams(
        vmem_limit_bytes=mib * MIB, dimension_semantics=("arbitrary",)
    )


def cost(flops, bytes_accessed):
    return pl.CostEstimate(
        flops=int(flops), bytes_accessed=int(bytes_accessed), transcendentals=0
    )


ORDERED = ROWS + 16 * OWNERS
ID_ROWS = 8


def rank_rows(owner, lists):
    owner_hot = (owner == lax.broadcasted_iota(I32, (OWNERS, ROWS), 0)).astype(F32)
    before = (
        lax.broadcasted_iota(I32, (128, 128), 0) < lax.broadcasted_iota(I32, (128, 128), 1)
    ).astype(F32)
    blocks = ROWS // 128
    stacked = jnp.concatenate(
        [owner_hot[:, b * 128 : (b + 1) * 128] for b in range(blocks)], axis=0
    ).astype(BF)
    inside = nn(stacked, before.astype(BF))
    ranks = []
    carry = jnp.zeros((OWNERS, 1), F32)
    for b in range(blocks):
        hot = owner_hot[:, b * 128 : (b + 1) * 128]
        earlier = inside[b * OWNERS : (b + 1) * OWNERS] + carry
        ranks.append(jnp.sum(hot * earlier, axis=0, keepdims=True))
        carry = carry + jnp.sum(hot, axis=1, keepdims=True)
    rank = jnp.concatenate(ranks, axis=1)
    pages = ((carry.astype(I32) + 15) // 16).astype(F32).astype(BF)
    after = before[:OWNERS, :OWNERS].T.astype(BF)
    first = nn(after, jnp.broadcast_to(pages, (OWNERS, 128)))
    begin = jnp.sum(owner_hot * first[:, :1], axis=0, keepdims=True) * 16.0
    place = (begin + rank).astype(I32)
    rank = rank.astype(I32)
    rank_hot = (rank == lax.broadcasted_iota(I32, (CAP, ROWS), 0)).astype(F32).astype(BF)
    high = (lists // 128).astype(F32)
    low = (lists % 128).astype(F32)
    left = jnp.concatenate([owner_hot * high, owner_hot * low, owner_hot], axis=0).astype(BF)
    found = nt(left, rank_hot)
    number = found[:OWNERS] * 128.0 + found[OWNERS : 2 * OWNERS]
    ids = (number + found[2 * OWNERS :] - 1.0).astype(I32)
    return place, first.astype(I32), ids


def order_rows(place, rot_ref, run_ref, row_steps, chunks):
    run_rows = ORDERED // row_steps
    one = jnp.ones((), BF)
    zero = jnp.zeros((), BF)
    digit = lax.broadcasted_iota(I32, (run_rows, ROWS), 0).astype(I16)
    for k in chunks:
        hot = jnp.where((place - k * run_rows).astype(I16) == digit, one, zero)
        run_ref[k * run_rows : (k + 1) * run_rows, :] = nn(hot, rot_ref[...]).astype(BF)


def route_kernel(half, parts, row_steps, step_owners, *refs):
    if half == 0:
        owner_ref, list_ref, rows_hbm, matrix_hbm, out_ref, place_ref, first_ref = refs[:7]
        start_ref, ids_ref, rows_ref, matrix_ref, rot_ref, run_ref, in_sem, matrix_sem, start_sem = refs[7:]
    else:
        start_ref, place_ref, rows_hbm, matrix_hbm, out_ref = refs[:5]
        rows_ref, matrix_ref, rot_ref, run_ref, in_sem, matrix_sem = refs[5:]
    step = pl.program_id(0)
    part_rows = ROWS // parts

    @pl.when(step == 0)
    def _():
        columns = []
        for g in range(GROUPS):
            columns.append(
                pltpu.make_async_copy(
                    matrix_hbm.at[:, pl.ds((2 * g + half) * 128, 128)],
                    matrix_ref.at[:, pl.ds(g * 128, 128)],
                    matrix_sem.at[g],
                )
            )
            columns[g].start()
        copies = []
        for k in range(parts):
            part = pl.ds(k * part_rows, part_rows)
            copies.append(
                pltpu.make_async_copy(rows_hbm.at[part], rows_ref.at[part], in_sem.at[k])
            )
            copies[k].start()
        if half == 0:
            place, first, ids = rank_rows(owner_ref[...], list_ref[...])
            place_ref[...] = place
            first_ref[...] = first
            ids_ref[...] = ids
            starts = pltpu.make_async_copy(first_ref, start_ref, start_sem)
            starts.start()
        rest = ORDERED + CAP - step_owners * CAP
        run_ref[step_owners * CAP :, :] = jnp.zeros((rest, GROUPS * 128), BF)
        for copy in columns:
            copy.wait()
        for k in range(parts):
            part = pl.ds(k * part_rows, part_rows)
            copies[k].wait()
            rot_ref[part, :] = nn(rows_ref[part, :], matrix_ref[...]).astype(BF)
        if half == 0:
            starts.wait()

    needed = step_owners * CAP * row_steps // ORDERED
    for k in range(-(-row_steps // needed)):
        chunks = range(k * needed, min((k + 1) * needed, row_steps))

        @pl.when(step == k)
        def _(chunks=chunks):
            order_rows(place_ref[...], rot_ref, run_ref, row_steps, chunks)

    line = lax.broadcasted_iota(I32, (ID_ROWS, CAP), 0)
    for j in range(step_owners):
        owner = step * step_owners + j
        begin = pl.multiple_of(start_ref[owner, 0] * 16, 16)
        run = run_ref[pl.ds(begin, CAP), :]
        for g in range(GROUPS):
            out_ref[g, j, :CAP, :] = run[:, g * 128 : (g + 1) * 128]
        if half == 0:
            ids = ids_ref[pl.ds(owner, 1), :]
            high = jnp.where(ids < 0, -1, ids // 128)
            low = ids % 128
            tail = jnp.where(line == 0, high, jnp.where(line == 1, low, 0))
            tail = tail.astype(F32).astype(BF)
            for g in range(GROUPS):
                out_ref[g, j, CAP:, :] = tail


def route(half, first_arg, second_arg, embeddings, matrix):
    step_owners = 8
    parts = 2
    row_steps = 5
    depth = CAP + (ID_ROWS if half == 0 else 0)
    line = pl.BlockSpec((1, ROWS), lambda i: (0, 0))
    out_specs = [pl.BlockSpec((GROUPS, step_owners, depth, 128), lambda i: (0, i, 0, 0))]
    out_shape = [jax.ShapeDtypeStruct((GROUPS, OWNERS, depth, 128), BF)]
    scratch = [
        pltpu.VMEM((ROWS, WIDTH), BF),
        pltpu.VMEM((WIDTH, GROUPS * 128), BF),
        pltpu.VMEM((ROWS, GROUPS * 128), BF),
        pltpu.VMEM((ORDERED + CAP, GROUPS * 128), BF),
        pltpu.SemaphoreType.DMA((parts,)),
        pltpu.SemaphoreType.DMA((GROUPS,)),
    ]
    if half == 0:
        inputs = [line, line]
        out_specs += [line, pl.BlockSpec((OWNERS, 128), lambda i: (0, 0))]
        out_shape += [
            jax.ShapeDtypeStruct((1, ROWS), I32),
            jax.ShapeDtypeStruct((OWNERS, 128), I32),
        ]
        scratch = [
            pltpu.SMEM((OWNERS, 128), I32),
            pltpu.VMEM((OWNERS, CAP), I32),
            *scratch,
            pltpu.SemaphoreType.DMA,
        ]
    else:
        inputs = [pl.BlockSpec(memory_space=pltpu.SMEM), line]
    return pl.pallas_call(
        functools.partial(route_kernel, half, parts, row_steps, step_owners),
        grid=(OWNERS // step_owners,),
        in_specs=[*inputs, pl.BlockSpec(memory_space=pl.ANY), pl.BlockSpec(memory_space=pl.ANY)],
        out_specs=out_specs,
        out_shape=out_shape,
        scratch_shapes=scratch,
        compiler_params=params(60),
        cost_estimate=cost(8e9, 10 * MIB),
    )(first_arg, second_arg, embeddings, matrix)


def pick_kernel(step_sources, tail_ref, centroid_ref, out_ref, ids_ref):
    one = jnp.ones((), BF)
    zero = jnp.zeros((), BF)
    lane = lax.broadcasted_iota(I32, (CAP, 128), 1).astype(I16)
    numbers = []
    hots = []
    for j in range(step_sources):
        tail = tail_ref[j, CAP:, :].astype(F32)
        number = tail[0:1, :] * 128.0 + tail[1:2, :]
        numbers.append(number)
        column = jnp.broadcast_to(number, (128, CAP)).T.astype(I32).astype(I16)
        hots.append(
            jnp.concatenate(
                [
                    jnp.where(column == lane + jnp.int16(128 * b), one, zero)
                    for b in range(LISTS // 128)
                ],
                axis=1,
            )
        )
    found = nn(jnp.concatenate(hots, axis=0), centroid_ref[...]).astype(BF)
    out_ref[...] = found.reshape(step_sources, CAP, 256)
    ids_ref[...] = jnp.concatenate(numbers, axis=1)


def pick(rows0, centroids):
    step_sources = 16
    slots = step_sources * CAP
    return pl.pallas_call(
        functools.partial(pick_kernel, step_sources),
        grid=(SOURCES // step_sources,),
        in_specs=[
            pl.BlockSpec((step_sources, CAP + ID_ROWS, CAP), lambda i: (i, 0, 0)),
            pl.BlockSpec((LISTS, 256), lambda i: (0, 0)),
        ],
        out_specs=[
            pl.BlockSpec((step_sources, CAP, 256), lambda i: (i, 0, 0)),
            pl.BlockSpec((1, slots), lambda i: (0, i)),
        ],
        out_shape=[
            jax.ShapeDtypeStruct((SOURCES, CAP, 256), BF),
            jax.ShapeDtypeStruct((1, SLOTS), F32),
        ],
        compiler_params=params(60),
        cost_estimate=cost(18e9, 14 * MIB),
    )(rows0, centroids)


def book_kernel(code_ref, out_ref):
    codes = code_ref[...].astype(F32).T
    lane = lax.broadcasted_iota(I32, (CODES, 128), 1)
    for m in range(8):
        mine = jnp.where(lane // 16 == m, codes, 0.0)
        square = jnp.sum(mine * mine, axis=1, keepdims=True)
        high = square.astype(BF).astype(F32)
        middle = (square - high).astype(BF).astype(F32)
        low = square - high - middle
        tail = jnp.where(
            lane == 0, high, jnp.where(lane == 1, middle, jnp.where(lane == 2, low, 0.0))
        )
        out_ref[m * CODES : (m + 1) * CODES, :128] = (-2.0 * mine).astype(BF)
        out_ref[m * CODES : (m + 1) * CODES, 128:] = tail.astype(BF)


def make_book(codebook):
    return pl.pallas_call(
        book_kernel,
        grid=(2,),
        in_specs=[pl.BlockSpec((128, CODES), lambda i: (i, 0))],
        out_specs=pl.BlockSpec((8 * CODES, 256), lambda i: (i, 0)),
        out_shape=jax.ShapeDtypeStruct((16 * CODES, 256), BF),
        compiler_params=params(60),
        cost_estimate=cost(1e9, 3 * MIB),
    )(codebook.reshape(256, CODES))


def residual(rows_ref, pick_ref, slots):
    rows = rows_ref[...].reshape(slots, 128).astype(F32)
    centre = pick_ref[...].reshape(slots, 128).astype(F32)
    return (rows - centre).astype(BF)


def add_sums(slots, flipped, live, target, acc_ref):
    high = jnp.where(live, target // 64, -1).astype(I16)
    low = (target % 64).astype(I16)
    digit = lax.broadcasted_iota(I32, (64, slots), 0).astype(I16)
    line = lax.broadcasted_iota(I32, (16, slots), 0)
    nth = (line // 4).astype(I16)
    quarter = (line % 4).astype(I16)
    one = jnp.ones((), BF)
    zero = jnp.zeros((), BF)
    for t in range(2):
        left = []
        right = []
        mixed = jnp.zeros((16, slots), I16)
        for m in range(4 * t, 4 * t + 4):
            mine = flipped[m * 16 : (m + 1) * 16]
            row = jnp.broadcast_to(high[m : m + 1], (16, slots))
            mixed = jnp.where(nth == jnp.int16(m % 4), row, mixed)
            for h in range(4):
                left.append(jnp.where(row == jnp.int16(h), mine, zero))
            right.append(jnp.where(low[m : m + 1] == digit, one, zero))
        left.append(jnp.where(mixed == quarter, one, zero))
        acc_ref[t] += nt(jnp.concatenate(left, axis=0), jnp.concatenate(right, axis=0))


def sum_of(acc_ref, m):
    base = (m % 4) * 64
    part = acc_ref[m // 4][:, base : base + 64]
    return jnp.concatenate([part[base + h * 16 : base + (h + 1) * 16] for h in range(4)], axis=1)


def count_of(acc_ref, m):
    base = (m % 4) * 64
    part = acc_ref[m // 4][256:, base : base + 64]
    at = (m % 4) * 4
    return jnp.concatenate([part[at + h : at + h + 1] for h in range(4)], axis=1)


def least_errors(slots, resid, flipped, live, book_ref):
    wide = jnp.concatenate([resid, jnp.ones((slots, 128), BF)], axis=1)
    lines = []
    for m in range(8):
        mine = flipped[m * 16 : (m + 1) * 16].astype(F32)
        row_sq = jnp.sum(mine * mine, axis=0, keepdims=True)
        dist = nt(book_ref[m * CODES : (m + 1) * CODES], wide)
        least = jnp.min(dist, axis=0, keepdims=True)
        lines.append(jnp.where(live, row_sq + least, 0.0))
    return lines


def half_specs(step_sources, half, begin=0):
    slots = step_sources * CAP
    return [
        pl.BlockSpec((step_sources, CAP, 128), lambda i: (i + begin, 0, 0)),
        pl.BlockSpec((step_sources, CAP, 128), lambda i: (i + begin, 0, half)),
        pl.BlockSpec((1, slots), lambda i: (0, i + begin)),
        pl.BlockSpec((8, slots), lambda i: (half, i + begin)),
        pl.BlockSpec((8 * CODES, 256), lambda i: (half, 0)),
    ]


def first_half_kernel(slots, rows_ref, pick_ref, ids_ref, target_ref, book_ref,
                      error_ref, sum_ref, count_ref, acc_ref):
    step = pl.program_id(0)

    @pl.when(step == 0)
    def _():
        acc_ref[...] = jnp.zeros_like(acc_ref)

    resid = residual(rows_ref, pick_ref, slots)
    flipped = resid.T
    live = ids_ref[...] >= 0
    add_sums(slots, flipped, live, target_ref[...], acc_ref)
    for m, line in enumerate(least_errors(slots, resid, flipped, live, book_ref)):
        error_ref[m : m + 1, :] = line

    @pl.when(step == pl.num_programs(0) - 1)
    def _():
        for m in range(8):
            sum_ref[m] = sum_of(acc_ref, m)
            count_ref[m : m + 1, :] = count_of(acc_ref, m)


def first_half(rows, picked, ids, targets, book):
    step_sources = 32
    slots = step_sources * CAP
    return pl.pallas_call(
        functools.partial(first_half_kernel, slots),
        grid=(SOURCES // step_sources,),
        in_specs=half_specs(step_sources, 0),
        out_specs=[
            pl.BlockSpec((8, slots), lambda i: (0, i)),
            pl.BlockSpec((8, 16, CODES), lambda i: (0, 0, 0)),
            pl.BlockSpec((8, CODES), lambda i: (0, 0)),
        ],
        out_shape=[
            jax.ShapeDtypeStruct((16, SLOTS), F32),
            jax.ShapeDtypeStruct((8, 16, CODES), F32),
            jax.ShapeDtypeStruct((8, CODES), F32),
        ],
        scratch_shapes=[pltpu.VMEM((2, 272, 256), F32)],
        compiler_params=params(60),
        cost_estimate=cost(22e9, 10 * MIB),
    )(rows, picked, ids, targets, book)


def last_sums_kernel(slots, rows_ref, pick_ref, ids_ref, target_ref, sum_ref, count_ref, out_ref, acc_ref):
    step = pl.program_id(0)

    @pl.when(step == 0)
    def _():
        acc_ref[...] = jnp.zeros_like(acc_ref)
        out_ref[:, 16:, :] = jnp.zeros((OWNERS, 8, 128), F32)

    resid = residual(rows_ref, pick_ref, slots)
    flipped = resid.T
    add_sums(slots, flipped, ids_ref[...] >= 0, target_ref[...], acc_ref)

    @pl.when(step == pl.num_programs(0) - 1)
    def _():
        for m in range(16):
            total = sum_ref[m] if m < 8 else sum_of(acc_ref, m - 8)
            count = count_ref[m : m + 1, :] if m < 8 else count_of(acc_ref, m - 8)
            for h in range(2):
                out_ref[2 * m + h, :8, :] = total[8 * h : 8 * h + 8, :128]
                out_ref[2 * m + h, 8:16, :] = total[8 * h : 8 * h + 8, 128:]
                out_ref[2 * m + h, 16:17, :] = count[:, :128]
                out_ref[2 * m + h, 17:18, :] = count[:, 128:]


def last_sums(rows, picked, ids, targets, sums, counts):
    step_sources = 32
    slots = step_sources * CAP
    return pl.pallas_call(
        functools.partial(last_sums_kernel, slots),
        grid=(SOURCES // step_sources,),
        in_specs=[
            *half_specs(step_sources, 1)[:4],
            pl.BlockSpec((8, 16, CODES), lambda i: (0, 0, 0)),
            pl.BlockSpec((8, CODES), lambda i: (0, 0)),
        ],
        out_specs=pl.BlockSpec((OWNERS, 24, 128), lambda i: (0, 0, 0)),
        out_shape=jax.ShapeDtypeStruct((OWNERS, 24, 128), F32),
        scratch_shapes=[pltpu.VMEM((2, 272, 256), F32)],
        compiler_params=params(60),
        cost_estimate=cost(4e9, 9 * MIB),
    )(rows, picked, ids, targets, sums, counts)


def last_errors_kernel(slots, rows_ref, pick_ref, ids_ref, book_ref, before_ref, out_ref):
    del before_ref
    blocks = 4
    part = slots // blocks
    for b in range(blocks):
        sources = slice(b * part // CAP, (b + 1) * part // CAP)
        at = slice(b * part, (b + 1) * part)
        resid = residual(rows_ref.at[sources], pick_ref.at[sources], part)
        live = ids_ref[:, at] >= 0
        for m, line in enumerate(least_errors(part, resid, resid.T, live, book_ref)):
            out_ref[m : m + 1, at] = line


def last_errors(begin, end, rows, picked, ids, book, before):
    step_sources = 32
    slots = step_sources * CAP
    specs = half_specs(step_sources, 1, begin)
    return pl.pallas_call(
        functools.partial(last_errors_kernel, slots),
        grid=(end - begin,),
        in_specs=[*specs[:3], specs[4], pl.BlockSpec(memory_space=pl.ANY)],
        out_specs=pl.BlockSpec((8, slots), lambda i: (1, i + begin)),
        out_shape=jax.ShapeDtypeStruct((16, SLOTS), F32),
        input_output_aliases={4: 0},
        compiler_params=params(60),
        cost_estimate=cost(4.4e9 * (end - begin), (end - begin) * 3 * MIB),
    )(rows, picked, ids, book, before)


def new_piece(got, codes):
    total = jnp.sum(got, axis=0)
    low = (codes[:, :128] + total[:8]) / (1.0 + total[16:17])
    high = (codes[:, 128:] + total[8:16]) / (1.0 + total[17:18])
    piece = jnp.concatenate([low, high], axis=1)
    return jnp.broadcast_to(piece[None], (OWNERS, 8, CODES))


def exchange(x, axes):
    return lax.all_to_all(x, axes, split_axis=0, concat_axis=0, tiled=True)


def per_device(
    embeddings, owner_of_row, list_in_owner, opq_matrix, centroids, codebook, code_targets
):
    every = ("sub", "lists")
    owner = owner_of_row.reshape(1, ROWS)
    lists = list_in_owner.reshape(1, ROWS)
    send0, place, start = route(0, owner, lists, embeddings, opq_matrix)
    rows0 = exchange(send0.reshape(SOURCES, CAP + ID_ROWS, 128), every)
    (send1,) = route(1, start, place, embeddings, opq_matrix)
    book = make_book(codebook)
    me = lax.axis_index("lists")
    codes = codebook.astype(F32).reshape(OWNERS, 8, CODES)
    codes = lax.dynamic_slice(codes, (me, 0, 0), (1, 8, CODES))[0]
    send1, book, codes = lax.optimization_barrier((send1, book, codes))
    rows1 = exchange(send1.reshape(SOURCES, CAP, 128), every)
    picked, ids = pick(rows0, centroids)
    quant_error, sums, counts = first_half(rows0, picked, ids, code_targets, book)
    rows1, quant_error, sums = lax.optimization_barrier((rows1, quant_error, sums))
    pieces = last_sums(rows1, picked, ids, code_targets, sums, counts)
    quant_error = last_errors(0, 2, rows1, picked, ids, book, quant_error)
    got = exchange(pieces, "lists")
    piece, quant_error = lax.optimization_barrier((new_piece(got, codes), quant_error))
    spread = exchange(piece, "lists")
    quant_error = last_errors(2, 4, rows1, picked, ids, book, quant_error)
    return quant_error, spread.reshape(16, 16, CODES)


def solution(mesh):
    placed = (
        P(("lists", "sub"), None),
        P(("lists", "sub"), None),
        P(("lists", "sub")),
        P(),
        P("lists", "sub"),
        P("sub", None, None),
        P("sub", "lists"),
    )
    return jax.shard_map(
        per_device,
        mesh=mesh,
        in_specs=placed,
        out_specs=(P("sub", "lists"), P("sub", None, None)),
        check_vma=False,
    )
```

```python
import functools

import jax
import jax.numpy as jnp
from jax import lax
from jax.experimental import pallas as pl
from jax.experimental.pallas import tpu as pltpu
from jax.sharding import PartitionSpec as P

BF = jnp.bfloat16
F32 = jnp.float32
I32 = jnp.int32
I16 = jnp.int16
OWNERS = 32
GROUPS = 4
CAP = 128
ROWS = 2048
WIDTH = 1024
SOURCES = OWNERS * GROUPS
SLOTS = SOURCES * CAP
LISTS = 2048
CODES = 256
MIB = 2**20


def nn(a, b):
    return jnp.dot(a, b, preferred_element_type=F32)


def nt(a, b):
    return lax.dot_general(a, b, (((1,), (1,)), ((), ())), preferred_element_type=F32)


def params(mib):
    return pltpu.CompilerParams(
        vmem_limit_bytes=mib * MIB, dimension_semantics=("arbitrary",)
    )


def cost(flops, bytes_accessed):
    return pl.CostEstimate(
        flops=int(flops), bytes_accessed=int(bytes_accessed), transcendentals=0
    )


ORDERED = ROWS + 16 * OWNERS
ID_ROWS = 8


def rank_rows(owner, lists):
    owner_hot = (owner == lax.broadcasted_iota(I32, (OWNERS, ROWS), 0)).astype(F32)
    before = (
        lax.broadcasted_iota(I32, (128, 128), 0) < lax.broadcasted_iota(I32, (128, 128), 1)
    ).astype(F32)
    blocks = ROWS // 128
    stacked = jnp.concatenate(
        [owner_hot[:, b * 128 : (b + 1) * 128] for b in range(blocks)], axis=0
    ).astype(BF)
    inside = nn(stacked, before.astype(BF))
    ranks = []
    carry = jnp.zeros((OWNERS, 1), F32)
    for b in range(blocks):
        hot = owner_hot[:, b * 128 : (b + 1) * 128]
        earlier = inside[b * OWNERS : (b + 1) * OWNERS] + carry
        ranks.append(jnp.sum(hot * earlier, axis=0, keepdims=True))
        carry = carry + jnp.sum(hot, axis=1, keepdims=True)
    rank = jnp.concatenate(ranks, axis=1)
    pages = ((carry.astype(I32) + 15) // 16).astype(F32).astype(BF)
    after = before[:OWNERS, :OWNERS].T.astype(BF)
    first = nn(after, jnp.broadcast_to(pages, (OWNERS, 128)))
    begin = jnp.sum(owner_hot * first[:, :1], axis=0, keepdims=True) * 16.0
    place = (begin + rank).astype(I32)
    rank = rank.astype(I32)
    rank_hot = (rank == lax.broadcasted_iota(I32, (CAP, ROWS), 0)).astype(F32).astype(BF)
    high = (lists // 128).astype(F32)
    low = (lists % 128).astype(F32)
    left = jnp.concatenate([owner_hot * high, owner_hot * low, owner_hot], axis=0).astype(BF)
    found = nt(left, rank_hot)
    number = found[:OWNERS] * 128.0 + found[OWNERS : 2 * OWNERS]
    ids = (number + found[2 * OWNERS :] - 1.0).astype(I32)
    return place, first.astype(I32), ids


def order_rows(place, rot_ref, run_ref, row_steps, chunks):
    run_rows = ORDERED // row_steps
    one = jnp.ones((), BF)
    zero = jnp.zeros((), BF)
    digit = lax.broadcasted_iota(I32, (run_rows, ROWS), 0).astype(I16)
    for k in chunks:
        hot = jnp.where((place - k * run_rows).astype(I16) == digit, one, zero)
        run_ref[k * run_rows : (k + 1) * run_rows, :] = nn(hot, rot_ref[...]).astype(BF)


def route_kernel(half, parts, row_steps, step_owners, *refs):
    if half == 0:
        owner_ref, list_ref, rows_hbm, matrix_hbm, out_ref, place_ref, first_ref = refs[:7]
        start_ref, ids_ref, rows_ref, matrix_ref, rot_ref, run_ref, in_sem, matrix_sem, start_sem = refs[7:]
    else:
        start_ref, place_ref, rows_hbm, matrix_hbm, out_ref = refs[:5]
        rows_ref, matrix_ref, rot_ref, run_ref, in_sem, matrix_sem = refs[5:]
    step = pl.program_id(0)
    part_rows = ROWS // parts

    @pl.when(step == 0)
    def _():
        columns = []
        for g in range(GROUPS):
            columns.append(
                pltpu.make_async_copy(
                    matrix_hbm.at[:, pl.ds((2 * g + half) * 128, 128)],
                    matrix_ref.at[:, pl.ds(g * 128, 128)],
                    matrix_sem.at[g],
                )
            )
            columns[g].start()
        copies = []
        for k in range(parts):
            part = pl.ds(k * part_rows, part_rows)
            copies.append(
                pltpu.make_async_copy(rows_hbm.at[part], rows_ref.at[part], in_sem.at[k])
            )
            copies[k].start()
        if half == 0:
            place, first, ids = rank_rows(owner_ref[...], list_ref[...])
            place_ref[...] = place
            first_ref[...] = first
            ids_ref[...] = ids
            starts = pltpu.make_async_copy(first_ref, start_ref, start_sem)
            starts.start()
        rest = ORDERED + CAP - step_owners * CAP
        run_ref[step_owners * CAP :, :] = jnp.zeros((rest, GROUPS * 128), BF)
        for copy in columns:
            copy.wait()
        for k in range(parts):
            part = pl.ds(k * part_rows, part_rows)
            copies[k].wait()
            rot_ref[part, :] = nn(rows_ref[part, :], matrix_ref[...]).astype(BF)
        if half == 0:
            starts.wait()

    needed = step_owners * CAP * row_steps // ORDERED
    for k in range(-(-row_steps // needed)):
        chunks = range(k * needed, min((k + 1) * needed, row_steps))

        @pl.when(step == k)
        def _(chunks=chunks):
            order_rows(place_ref[...], rot_ref, run_ref, row_steps, chunks)

    line = lax.broadcasted_iota(I32, (ID_ROWS, CAP), 0)
    for j in range(step_owners):
        owner = step * step_owners + j
        begin = pl.multiple_of(start_ref[owner, 0] * 16, 16)
        run = run_ref[pl.ds(begin, CAP), :]
        for g in range(GROUPS):
            out_ref[g, j, :CAP, :] = run[:, g * 128 : (g + 1) * 128]
        if half == 0:
            ids = ids_ref[pl.ds(owner, 1), :]
            high = jnp.where(ids < 0, -1, ids // 128)
            low = ids % 128
            tail = jnp.where(line == 0, high, jnp.where(line == 1, low, 0))
            tail = tail.astype(F32).astype(BF)
            for g in range(GROUPS):
                out_ref[g, j, CAP:, :] = tail


def route(half, first_arg, second_arg, embeddings, matrix):
    step_owners = 8
    parts = 2
    row_steps = 10
    depth = CAP + (ID_ROWS if half == 0 else 0)
    line = pl.BlockSpec((1, ROWS), lambda i: (0, 0))
    out_specs = [pl.BlockSpec((GROUPS, step_owners, depth, 128), lambda i: (0, i, 0, 0))]
    out_shape = [jax.ShapeDtypeStruct((GROUPS, OWNERS, depth, 128), BF)]
    scratch = [
        pltpu.VMEM((ROWS, WIDTH), BF),
        pltpu.VMEM((WIDTH, GROUPS * 128), BF),
        pltpu.VMEM((ROWS, GROUPS * 128), BF),
        pltpu.VMEM((ORDERED + CAP, GROUPS * 128), BF),
        pltpu.SemaphoreType.DMA((parts,)),
        pltpu.SemaphoreType.DMA((GROUPS,)),
    ]
    if half == 0:
        inputs = [line, line]
        out_specs += [line, pl.BlockSpec((OWNERS, 128), lambda i: (0, 0))]
        out_shape += [
            jax.ShapeDtypeStruct((1, ROWS), I32),
            jax.ShapeDtypeStruct((OWNERS, 128), I32),
        ]
        scratch = [
            pltpu.SMEM((OWNERS, 128), I32),
            pltpu.VMEM((OWNERS, CAP), I32),
            *scratch,
            pltpu.SemaphoreType.DMA,
        ]
    else:
        inputs = [pl.BlockSpec(memory_space=pltpu.SMEM), line]
    return pl.pallas_call(
        functools.partial(route_kernel, half, parts, row_steps, step_owners),
        grid=(OWNERS // step_owners,),
        in_specs=[*inputs, pl.BlockSpec(memory_space=pl.ANY), pl.BlockSpec(memory_space=pl.ANY)],
        out_specs=out_specs,
        out_shape=out_shape,
        scratch_shapes=scratch,
        compiler_params=params(60),
        cost_estimate=cost(8e9, 10 * MIB),
    )(first_arg, second_arg, embeddings, matrix)


def pick_kernel(step_sources, tail_ref, centroid_ref, out_ref, ids_ref):
    one = jnp.ones((), BF)
    zero = jnp.zeros((), BF)
    lane = lax.broadcasted_iota(I32, (CAP, 128), 1).astype(I16)
    numbers = []
    hots = []
    for j in range(step_sources):
        tail = tail_ref[j, CAP:, :].astype(F32)
        number = tail[0:1, :] * 128.0 + tail[1:2, :]
        numbers.append(number)
        column = jnp.broadcast_to(number, (128, CAP)).T.astype(I32).astype(I16)
        hots.append(
            jnp.concatenate(
                [
                    jnp.where(column == lane + jnp.int16(128 * b), one, zero)
                    for b in range(LISTS // 128)
                ],
                axis=1,
            )
        )
    found = nn(jnp.concatenate(hots, axis=0), centroid_ref[...]).astype(BF)
    out_ref[...] = found.reshape(step_sources, CAP, 256)
    ids_ref[...] = jnp.concatenate(numbers, axis=1)


def pick(rows0, centroids):
    step_sources = 16
    slots = step_sources * CAP
    return pl.pallas_call(
        functools.partial(pick_kernel, step_sources),
        grid=(SOURCES // step_sources,),
        in_specs=[
            pl.BlockSpec((step_sources, CAP + ID_ROWS, CAP), lambda i: (i, 0, 0)),
            pl.BlockSpec((LISTS, 256), lambda i: (0, 0)),
        ],
        out_specs=[
            pl.BlockSpec((step_sources, CAP, 256), lambda i: (i, 0, 0)),
            pl.BlockSpec((1, slots), lambda i: (0, i)),
        ],
        out_shape=[
            jax.ShapeDtypeStruct((SOURCES, CAP, 256), BF),
            jax.ShapeDtypeStruct((1, SLOTS), F32),
        ],
        compiler_params=params(60),
        cost_estimate=cost(18e9, 14 * MIB),
    )(rows0, centroids)


def book_kernel(code_ref, out_ref):
    codes = code_ref[...].astype(F32).T
    lane = lax.broadcasted_iota(I32, (CODES, 128), 1)
    for m in range(8):
        mine = jnp.where(lane // 16 == m, codes, 0.0)
        square = jnp.sum(mine * mine, axis=1, keepdims=True)
        high = square.astype(BF).astype(F32)
        middle = (square - high).astype(BF).astype(F32)
        low = square - high - middle
        tail = jnp.where(
            lane == 0, high, jnp.where(lane == 1, middle, jnp.where(lane == 2, low, 0.0))
        )
        out_ref[m * CODES : (m + 1) * CODES, :128] = (-2.0 * mine).astype(BF)
        out_ref[m * CODES : (m + 1) * CODES, 128:] = tail.astype(BF)


def make_book(codebook):
    return pl.pallas_call(
        book_kernel,
        grid=(2,),
        in_specs=[pl.BlockSpec((128, CODES), lambda i: (i, 0))],
        out_specs=pl.BlockSpec((8 * CODES, 256), lambda i: (i, 0)),
        out_shape=jax.ShapeDtypeStruct((16 * CODES, 256), BF),
        compiler_params=params(60),
        cost_estimate=cost(1e9, 3 * MIB),
    )(codebook.reshape(256, CODES))


def residual(rows_ref, pick_ref, slots):
    rows = rows_ref[...].reshape(slots, 128).astype(F32)
    centre = pick_ref[...].reshape(slots, 128).astype(F32)
    return (rows - centre).astype(BF)


def add_sums(slots, flipped, live, target, acc_ref):
    high = jnp.where(live, target // 64, -1).astype(I16)
    low = (target % 64).astype(I16)
    digit = lax.broadcasted_iota(I32, (64, slots), 0).astype(I16)
    line = lax.broadcasted_iota(I32, (16, slots), 0)
    nth = (line // 4).astype(I16)
    quarter = (line % 4).astype(I16)
    one = jnp.ones((), BF)
    zero = jnp.zeros((), BF)
    for t in range(2):
        left = []
        right = []
        mixed = jnp.zeros((16, slots), I16)
        for m in range(4 * t, 4 * t + 4):
            mine = flipped[m * 16 : (m + 1) * 16]
            row = jnp.broadcast_to(high[m : m + 1], (16, slots))
            mixed = jnp.where(nth == jnp.int16(m % 4), row, mixed)
            for h in range(4):
                left.append(jnp.where(row == jnp.int16(h), mine, zero))
            right.append(jnp.where(low[m : m + 1] == digit, one, zero))
        left.append(jnp.where(mixed == quarter, one, zero))
        acc_ref[t] += nt(jnp.concatenate(left, axis=0), jnp.concatenate(right, axis=0))


def sum_of(acc_ref, m):
    base = (m % 4) * 64
    part = acc_ref[m // 4][:, base : base + 64]
    return jnp.concatenate([part[base + h * 16 : base + (h + 1) * 16] for h in range(4)], axis=1)


def count_of(acc_ref, m):
    base = (m % 4) * 64
    part = acc_ref[m // 4][256:, base : base + 64]
    at = (m % 4) * 4
    return jnp.concatenate([part[at + h : at + h + 1] for h in range(4)], axis=1)


def least_errors(slots, resid, flipped, live, book_ref):
    wide = jnp.concatenate([resid, jnp.ones((slots, 128), BF)], axis=1)
    lines = []
    for m in range(8):
        mine = flipped[m * 16 : (m + 1) * 16].astype(F32)
        row_sq = jnp.sum(mine * mine, axis=0, keepdims=True)
        dist = nt(book_ref[m * CODES : (m + 1) * CODES], wide)
        least = jnp.min(dist, axis=0, keepdims=True)
        lines.append(jnp.where(live, row_sq + least, 0.0))
    return lines


def half_specs(step_sources, half, begin=0):
    slots = step_sources * CAP
    return [
        pl.BlockSpec((step_sources, CAP, 128), lambda i: (i + begin, 0, 0)),
        pl.BlockSpec((step_sources, CAP, 128), lambda i: (i + begin, 0, half)),
        pl.BlockSpec((1, slots), lambda i: (0, i + begin)),
        pl.BlockSpec((8, slots), lambda i: (half, i + begin)),
        pl.BlockSpec((8 * CODES, 256), lambda i: (half, 0)),
    ]


def first_half_kernel(slots, rows_ref, pick_ref, ids_ref, target_ref, book_ref,
                      error_ref, sum_ref, count_ref, acc_ref):
    step = pl.program_id(0)

    @pl.when(step == 0)
    def _():
        acc_ref[...] = jnp.zeros_like(acc_ref)

    resid = residual(rows_ref, pick_ref, slots)
    flipped = resid.T
    live = ids_ref[...] >= 0
    add_sums(slots, flipped, live, target_ref[...], acc_ref)
    for m, line in enumerate(least_errors(slots, resid, flipped, live, book_ref)):
        error_ref[m : m + 1, :] = line

    @pl.when(step == pl.num_programs(0) - 1)
    def _():
        for m in range(8):
            sum_ref[m] = sum_of(acc_ref, m)
            count_ref[m : m + 1, :] = count_of(acc_ref, m)


def first_half(rows, picked, ids, targets, book):
    step_sources = 32
    slots = step_sources * CAP
    return pl.pallas_call(
        functools.partial(first_half_kernel, slots),
        grid=(SOURCES // step_sources,),
        in_specs=half_specs(step_sources, 0),
        out_specs=[
            pl.BlockSpec((8, slots), lambda i: (0, i)),
            pl.BlockSpec((8, 16, CODES), lambda i: (0, 0, 0)),
            pl.BlockSpec((8, CODES), lambda i: (0, 0)),
        ],
        out_shape=[
            jax.ShapeDtypeStruct((16, SLOTS), F32),
            jax.ShapeDtypeStruct((8, 16, CODES), F32),
            jax.ShapeDtypeStruct((8, CODES), F32),
        ],
        scratch_shapes=[pltpu.VMEM((2, 272, 256), F32)],
        compiler_params=params(60),
        cost_estimate=cost(22e9, 10 * MIB),
    )(rows, picked, ids, targets, book)


def last_sums_kernel(slots, rows_ref, pick_ref, ids_ref, target_ref, sum_ref, count_ref, out_ref, acc_ref):
    step = pl.program_id(0)

    @pl.when(step == 0)
    def _():
        acc_ref[...] = jnp.zeros_like(acc_ref)
        out_ref[:, 16:, :] = jnp.zeros((OWNERS, 8, 128), F32)

    resid = residual(rows_ref, pick_ref, slots)
    flipped = resid.T
    add_sums(slots, flipped, ids_ref[...] >= 0, target_ref[...], acc_ref)

    @pl.when(step == pl.num_programs(0) - 1)
    def _():
        for m in range(16):
            total = sum_ref[m] if m < 8 else sum_of(acc_ref, m - 8)
            count = count_ref[m : m + 1, :] if m < 8 else count_of(acc_ref, m - 8)
            for h in range(2):
                out_ref[2 * m + h, :8, :] = total[8 * h : 8 * h + 8, :128]
                out_ref[2 * m + h, 8:16, :] = total[8 * h : 8 * h + 8, 128:]
                out_ref[2 * m + h, 16:17, :] = count[:, :128]
                out_ref[2 * m + h, 17:18, :] = count[:, 128:]


def last_sums(rows, picked, ids, targets, sums, counts):
    step_sources = 32
    slots = step_sources * CAP
    return pl.pallas_call(
        functools.partial(last_sums_kernel, slots),
        grid=(SOURCES // step_sources,),
        in_specs=[
            *half_specs(step_sources, 1)[:4],
            pl.BlockSpec((8, 16, CODES), lambda i: (0, 0, 0)),
            pl.BlockSpec((8, CODES), lambda i: (0, 0)),
        ],
        out_specs=pl.BlockSpec((OWNERS, 24, 128), lambda i: (0, 0, 0)),
        out_shape=jax.ShapeDtypeStruct((OWNERS, 24, 128), F32),
        scratch_shapes=[pltpu.VMEM((2, 272, 256), F32)],
        compiler_params=params(60),
        cost_estimate=cost(4e9, 9 * MIB),
    )(rows, picked, ids, targets, sums, counts)


def last_errors_kernel(slots, rows_ref, pick_ref, ids_ref, book_ref, before_ref, out_ref):
    del before_ref
    blocks = 2
    part = slots // blocks
    for b in range(blocks):
        sources = slice(b * part // CAP, (b + 1) * part // CAP)
        at = slice(b * part, (b + 1) * part)
        resid = residual(rows_ref.at[sources], pick_ref.at[sources], part)
        live = ids_ref[:, at] >= 0
        for m, line in enumerate(least_errors(part, resid, resid.T, live, book_ref)):
            out_ref[m : m + 1, at] = line


def last_errors(begin, end, rows, picked, ids, book, before):
    step_sources = 16
    slots = step_sources * CAP
    specs = half_specs(step_sources, 1, begin)
    return pl.pallas_call(
        functools.partial(last_errors_kernel, slots),
        grid=(end - begin,),
        in_specs=[*specs[:3], specs[4], pl.BlockSpec(memory_space=pl.ANY)],
        out_specs=pl.BlockSpec((8, slots), lambda i: (1, i + begin)),
        out_shape=jax.ShapeDtypeStruct((16, SLOTS), F32),
        input_output_aliases={4: 0},
        compiler_params=params(60),
        cost_estimate=cost(2.2e9 * (end - begin), (end - begin) * 1.5 * MIB),
    )(rows, picked, ids, book, before)


def new_piece(got, codes):
    total = jnp.sum(got, axis=0)
    low = (codes[:, :128] + total[:8]) / (1.0 + total[16:17])
    high = (codes[:, 128:] + total[8:16]) / (1.0 + total[17:18])
    piece = jnp.concatenate([low, high], axis=1)
    return jnp.broadcast_to(piece[None], (OWNERS, 8, CODES))


def exchange(x, axes):
    return lax.all_to_all(x, axes, split_axis=0, concat_axis=0, tiled=True)


def per_device(
    embeddings, owner_of_row, list_in_owner, opq_matrix, centroids, codebook, code_targets
):
    every = ("sub", "lists")
    owner = owner_of_row.reshape(1, ROWS)
    lists = list_in_owner.reshape(1, ROWS)
    send0, place, start = route(0, owner, lists, embeddings, opq_matrix)
    rows0 = exchange(send0.reshape(SOURCES, CAP + ID_ROWS, 128), every)
    (send1,) = route(1, start, place, embeddings, opq_matrix)
    book = make_book(codebook)
    me = lax.axis_index("lists")
    codes = codebook.astype(F32).reshape(OWNERS, 8, CODES)
    codes = lax.dynamic_slice(codes, (me, 0, 0), (1, 8, CODES))[0]
    send1, book, codes = lax.optimization_barrier((send1, book, codes))
    rows1 = exchange(send1.reshape(SOURCES, CAP, 128), every)
    picked, ids = pick(rows0, centroids)
    quant_error, sums, counts = first_half(rows0, picked, ids, code_targets, book)
    rows1, quant_error, sums = lax.optimization_barrier((rows1, quant_error, sums))
    pieces = last_sums(rows1, picked, ids, code_targets, sums, counts)
    quant_error = last_errors(0, 4, rows1, picked, ids, book, quant_error)
    got = exchange(pieces, "lists")
    piece, quant_error = lax.optimization_barrier((new_piece(got, codes), quant_error))
    spread = exchange(piece, "lists")
    quant_error = last_errors(4, 8, rows1, picked, ids, book, quant_error)
    return quant_error, spread.reshape(16, 16, CODES)


def solution(mesh):
    placed = (
        P(("lists", "sub"), None),
        P(("lists", "sub"), None),
        P(("lists", "sub")),
        P(),
        P("lists", "sub"),
        P("sub", None, None),
        P("sub", "lists"),
    )
    return jax.shard_map(
        per_device,
        mesh=mesh,
        in_specs=placed,
        out_specs=(P("sub", "lists"), P("sub", None, None)),
        check_vma=False,
    )
```
